128 devices in a mesh: wide: 16 (over x, z), narrow: 8 (over y, core).
Axes of the slice: x: 4, y: 4, z: 4, core: 2. Of those that a mesh axis runs over, the one named last changes fastest.
Arguments:
- disp: bfloat16 [4096, 48, 256], P(('wide', 'narrow')), may hold values from -6 to 6
- loads: bfloat16 [4096, 48, 256], P(('wide', 'narrow')), may hold values from -6 to 6
- tiles: bfloat16 [16384, 256, 256], P(('wide', 'narrow')), may hold values from -0.375 to 0.375
- pair_fpatch: int32 [16384], P(('wide', 'narrow')), may hold values from 0 to 31
- pair_sdev: int32 [16384, 1], P(('wide', 'narrow')), may hold values from 0 to 127; in each aligned block of 128 rows (0 to 127, 128 to 255, ...) at most 2 rows name the same one
- pair_spatch: int32 [16384], P(('wide', 'narrow')), may hold values from 0 to 31
Outputs:
- face_disp: float32 [4096, 48, 256], P(('wide', 'narrow'))
- struct_loads: float32 [4096, 48, 256], P(('wide', 'narrow'))
The draws below stay inside these ranges and needn't reach their ends.
Inputs may be any that keep to these rules, and one draw needn't show every extreme that they name: `pair_sdev`: among the pairs of one device, at most 2 name the same structure device, and some device reaches 2.
All inputs are finite; a program needn't handle non-finite values.
Results may differ from the reference program's by a relative error of at most 0.0003.
Values may be sent and summed in bfloat16 or wider, within the bound.
No kernel may reach another device: no remote copies, remote signals or barrier semaphores. Data moves between devices by JAX's collectives and lax.ppermute only.
A program may use at most 192 MiB of HBM per device.

```python
import math
import jax
import jax.numpy as jnp
import numpy as np
from jax import lax

FACES = 256
NODES = 256
COLS = 48
PAIR_DEV = 128
FP_DEV = 32
SP_DEV = 32
CAP = 2
PAIRS = 16384
F_PATCHES = 4096
S_PATCHES = 4096
N_WIDE = 16
N_NARROW = 8
DEVICES = 128


def set_ends(entries, key, least, high):
    dims = entries.shape
    index_at = [jax.random.randint(jax.random.fold_in(key, axis), (), 0, dims[axis]) for axis in range(len(dims))]
    entries = entries.at[tuple(index_at)].set(least)
    longest = dims.index(max(dims))
    index_at[longest] = (index_at[longest] + 1) % dims[longest]
    return entries.at[tuple(index_at)].set(high)


def steps_of(own_key, extent, pieces, least, largest):
    loudness = 1.0
    for dim, blocks in pieces:
        heights = jax.random.uniform(jax.random.fold_in(jax.random.fold_in(own_key, 6), dim), (blocks,), jnp.float32, least / len(pieces), largest / len(pieces))
        loudness = loudness * jnp.repeat(jnp.exp(heights), extent[dim] // blocks).reshape((-1,) + (1,) * (len(extent) - 1 - dim))
    return loudness


def deal_out(rng, own, number, rows, amount, top, limit, slope):
    sequence = jax.random.permutation(rng, amount)
    crowded, ordinary = shares(amount, rows * top, limit, slope, True), shares(amount, rows * top, limit, slope, False)
    places = jnp.arange(amount)

    def named(sizes, offset_by):
        used = int((sizes > 0).sum())
        fixed = max(1, used // 4)
        shifted = fixed + (places - fixed + offset_by * (used - fixed)) % max(1, amount - fixed)
        return jnp.zeros((amount,), jnp.int32).at[sequence[jnp.where(places < fixed, places, shifted)]].set(jnp.asarray(sizes, jnp.int32))

    sizes = jnp.where(number % 4 == 0, named(crowded, number // 4), named(ordinary, number - number // 4 - 1))
    mixed = jax.random.permutation(jax.random.fold_in(own, 3), amount)
    source_of, taker = mixed[0:amount // 2 * 2:2], mixed[1:amount // 2 * 2:2]
    room = jnp.minimum(sizes[source_of] - 1, limit - sizes[taker]) // 2
    room = jnp.where((source_of == sequence[0]) | (taker == sequence[0]) | (sizes[taker] == 0), 0, jnp.maximum(room, 0))
    shifted = jax.random.randint(jax.random.fold_in(own, 4), (amount // 2,), 0, 1 << 20) % (room + 1)
    sizes = sizes.at[source_of].add(-shifted).at[taker].add(shifted)
    labels = jnp.searchsorted(jnp.cumsum(sizes), jnp.arange(rows * top), side="right").astype(jnp.int32)
    grid = labels.reshape(top, rows).T
    grid = grid[jax.random.permutation(jax.random.fold_in(own, 1), rows)]
    offset_by = jax.random.randint(jax.random.fold_in(own, 2), (rows, 1), 0, top)
    return jnp.take_along_axis(grid, (jnp.arange(top)[None, :] + offset_by) % top, axis=1)


def shares(number_of, total, bound, skew, full):
    portions = [(1 << 20) // math.isqrt(grade ** skew) + 1 for grade in range(1, number_of + 1)]
    largest = bound if full else min(bound, max(-(-total // number_of), total * portions[0] // sum(portions)))
    least = 1 if total - largest >= number_of - 1 else 0
    counts, rest = [largest] + [least] * (number_of - 1), total - largest - least * (number_of - 1)
    while rest > 0:
        candidates = [i for i in range(1, number_of) if counts[i] < largest] or [i for i in range(1, number_of) if counts[i] < bound]
        mass, left = sum([portions[i] for i in candidates]), rest
        for i in candidates:
            extra = min(bound - counts[i], max(1, left * portions[i] // mass), rest)
            counts[i] = counts[i] + extra
            rest = rest - extra
    return np.array(counts)


def gaussian(stream_key, extent, spread, bound, cuts=(), dtype=jnp.bfloat16):
    entries = spread * jax.random.normal(stream_key, extent, jnp.float32)
    if cuts:
        entries = entries * steps_of(stream_key, extent, cuts, -0.22, 0.18)
    return jnp.clip(entries, -bound, bound).astype(dtype)


def setup_inputs(seed: int = 0) -> dict:
    keys = jax.random.split(jax.random.key(seed), 7)
    disp = gaussian(keys[0], (S_PATCHES, COLS, NODES), 1.0, 6.0, ((0, 128),))
    loads = gaussian(keys[1], (F_PATCHES, COLS, FACES), 1.0, 6.0, ((0, 128),))
    tiles = gaussian(keys[2], (PAIRS, FACES, NODES), NODES ** -0.5, 0.375, ((0, 128),))
    pair_fpatch = set_ends(jax.random.randint(keys[3], (PAIRS,), 0, FP_DEV), jax.random.fold_in(keys[3], 1), 0, FP_DEV - 1).astype(jnp.int32)
    pair_sdev_keys = jax.random.split(jax.random.fold_in(keys[4], 1), PAIRS // PAIR_DEV)
    pair_sdev_turns = jax.random.permutation(jax.random.fold_in(keys[4], 3), PAIRS // PAIR_DEV)
    pair_sdev = jax.vmap(lambda own, number: deal_out(jax.random.fold_in(keys[4], 2), own, number, PAIR_DEV, DEVICES, 1, CAP, 2))(pair_sdev_keys, pair_sdev_turns).reshape((PAIRS, 1))
    pair_spatch = set_ends(jax.random.randint(keys[5], (PAIRS,), 0, SP_DEV), jax.random.fold_in(keys[5], 1), 0, SP_DEV - 1).astype(jnp.int32)
    return {"disp": disp, "loads": loads, "tiles": tiles, "pair_fpatch": pair_fpatch, "pair_sdev": pair_sdev, "pair_spatch": pair_spatch}


def reference(disp, loads, tiles, pair_fpatch, pair_sdev, pair_spatch):
    n_dev = N_WIDE * N_NARROW
    face_acc = jnp.zeros((FP_DEV * n_dev, COLS, FACES), jnp.float32)
    struct_acc = jnp.zeros((SP_DEV * n_dev, COLS, NODES), jnp.float32)
    blocks = (jnp.arange(n_dev).astype(jnp.int32),
              tiles.reshape(n_dev, PAIR_DEV, FACES, NODES),
              pair_fpatch.reshape(n_dev, PAIR_DEV),
              pair_sdev.reshape(n_dev, PAIR_DEV),
              pair_spatch.reshape(n_dev, PAIR_DEV))

    def step(carry, block):
        face_sum, struct_sum = carry
        owner, tile_block, fpatch, sdev, spatch = block
        fid = (owner * FP_DEV + fpatch).astype(jnp.int32)
        sid = (sdev * SP_DEV + spatch).astype(jnp.int32)
        tile_wide = tile_block.astype(jnp.float32)
        moved = disp[sid].astype(jnp.float32)
        face_part = jnp.einsum("pcn,pfn->pcf", moved, tile_wide, precision=lax.Precision.HIGHEST)
        pulled = loads[fid].astype(jnp.float32)
        load_part = jnp.einsum("pcf,pfn->pcn", pulled, tile_wide, precision=lax.Precision.HIGHEST)
        return (face_sum.at[fid].add(face_part), struct_sum.at[sid].add(load_part)), None

    (face_disp, struct_loads), _ = lax.scan(step, (face_acc, struct_acc), blocks)
    return face_disp, struct_loads
```

```python
import functools

import jax
import jax.numpy as jnp
from jax import lax
from jax.experimental import pallas as pl
from jax.experimental.pallas import tpu as pltpu
from jax.sharding import PartitionSpec as P

ROOM = 12
META = 16
SHIFT = 4
GROUP = 8
DEPTH = 4
STEPS = 128.0
TOP = 32760.0


def long_way(disp, loads, tiles, pair_fpatch, pair_sdev, pair_spatch):
    n_wide = lax.axis_size("wide")
    n_narrow = lax.axis_size("narrow")
    n_dev = n_wide * n_narrow
    pair_count = tiles.shape[0]
    capacity = max(2, 2 * pair_count // n_dev)
    slot_count = n_dev * capacity
    columns = disp.shape[1]
    node_count = disp.shape[2]
    face_count = loads.shape[2]
    target = pair_sdev
    same_target = target[:, None] == target[None, :]
    earlier = lax.broadcasted_iota(jnp.int32, (pair_count, pair_count), 0) > lax.broadcasted_iota(
        jnp.int32, (pair_count, pair_count), 1
    )
    place = jnp.sum((same_target & earlier).astype(jnp.int32), axis=1)
    slot_of_pair = target * capacity + place
    hits = slot_of_pair[None, :] == jnp.arange(slot_count, dtype=jnp.int32)[:, None]
    filled = jnp.any(hits, axis=1)
    pair_of_slot = jnp.sum(
        jnp.where(hits, jnp.arange(pair_count, dtype=jnp.int32)[None, :], 0), axis=1
    )
    request = jnp.where(filled, pair_spatch[pair_of_slot], -1).reshape(n_dev, capacity)
    asked = lax.all_to_all(request, ("wide", "narrow"), split_axis=0, concat_axis=0, tiled=True)
    wanted = asked >= 0
    picked = disp[jnp.maximum(asked, 0)]
    answer = jnp.where(wanted[:, :, None, None], picked, jnp.zeros_like(picked))
    arrived = lax.all_to_all(answer, ("wide", "narrow"), split_axis=0, concat_axis=0, tiled=True)
    arrived = arrived.reshape(slot_count, columns, node_count)
    moved = arrived[slot_of_pair]
    face_part = jnp.einsum("pcn,pfn->pcf", moved, tiles, preferred_element_type=jnp.float32)
    fluid_onehot = (
        pair_fpatch[None, :] == jnp.arange(loads.shape[0], dtype=jnp.int32)[:, None]
    ).astype(jnp.float32)
    face_disp = jnp.dot(
        fluid_onehot,
        face_part.reshape(pair_count, -1),
        precision=lax.Precision.HIGHEST,
        preferred_element_type=jnp.float32,
    ).reshape(loads.shape[0], columns, face_count)
    pulled = loads[pair_fpatch]
    load_part = jnp.einsum("pcf,pfn->pcn", pulled, tiles, preferred_element_type=jnp.float32)
    outgoing = jnp.where(filled[:, None, None], load_part[pair_of_slot], 0.0).reshape(
        n_dev, capacity, columns, node_count
    )
    returned = lax.all_to_all(outgoing, ("wide", "narrow"), split_axis=0, concat_axis=0, tiled=True)
    returned = returned.reshape(slot_count, columns * node_count)
    struct_onehot = (
        asked.reshape(-1)[None, :] == jnp.arange(disp.shape[0], dtype=jnp.int32)[:, None]
    ).astype(jnp.float32)
    struct_loads = jnp.dot(
        struct_onehot, returned, precision=lax.Precision.HIGHEST, preferred_element_type=jnp.float32
    ).reshape(disp.shape[0], columns, node_count)
    return (face_disp, struct_loads)


def stream_tiles(tiles, buf, sems, body):
    groups = tiles.shape[0] // GROUP

    def copy(g):
        at = lax.rem(g, DEPTH)
        return pltpu.make_async_copy(tiles.at[pl.ds(g * GROUP, GROUP)], buf.at[at], sems.at[at])

    for g in range(DEPTH - 1):
        copy(g).start()

    def step(g, carry):
        @pl.when(g + DEPTH - 1 < groups)
        def _():
            copy(g + DEPTH - 1).start()

        copy(g).wait()
        at = lax.rem(g, DEPTH)
        for i in range(GROUP):
            body(g * GROUP + i, buf.at[at, i])
        return carry

    lax.fori_loop(0, groups, step, 0)


def send_kernel(n_narrow, fpatch, sdev, spatch, loads, tiles, disp, out, slot, aug, buf, meta, flag, count, sems, side):
    n_wide, patches, columns = out.shape[0], disp.shape[0], disp.shape[1]
    keep = pltpu.make_async_copy(disp, aug.at[pl.ds(0, patches)], side)
    keep.start()
    meta[...] = jnp.zeros_like(meta)
    for w in range(n_wide):
        count[w] = 0
        meta[w, ROOM : ROOM + 1, :] = jnp.full((1, meta.shape[2]), -1, jnp.int32)
    lane = lax.broadcasted_iota(jnp.int32, (1, meta.shape[2]), 1)

    def body(p, tile):
        target = sdev[p]
        w = target // n_narrow
        asked = (target - w * n_narrow) * patches + spatch[p]
        seen = count[w]
        count[w] = seen + 1
        place = jnp.minimum(seen, ROOM - 1)
        slot[p] = (w << SHIFT) | place
        part = jnp.dot(loads[fpatch[p]], tile[...], preferred_element_type=jnp.float32)
        most = jnp.maximum(jnp.max(jnp.abs(part), axis=0, keepdims=True), 1e-33)
        power = jnp.ceil(jnp.log2(most) * STEPS)
        unit = TOP * jnp.exp2(power * (-1.0 / STEPS))
        whole = jnp.clip(jnp.round(part * unit), -32767.0, 32767.0).astype(jnp.int32)
        out[w, pl.ds(pl.multiple_of(place * columns, 16), columns), :] = whole.astype(jnp.int16)
        meta[w, pl.ds(place, 1), :] = power.astype(jnp.int32)
        names = meta[w, ROOM : ROOM + 1, :]
        meta[w, ROOM : ROOM + 1, :] = jnp.where(lane == place, asked, names)

    stream_tiles(tiles, buf, sems, body)
    out[:, ROOM * columns :, :] = meta[...].astype(jnp.int16)
    fullest = count[0]
    for w in range(1, n_wide):
        fullest = jnp.maximum(fullest, count[w])
    flag[...] = jnp.full(flag.shape, fullest.astype(jnp.float32), jnp.float32).astype(flag.dtype)
    keep.wait()
    mark = pltpu.make_async_copy(flag, aug.at[pl.ds(patches, 1)], side)
    mark.start()
    mark.wait()


def turn_kernel(n_narrow, names, arrived, table, total, answer, acc, scale, flags, lists, count, picks, marks, outs):
    n_wide, columns = arrived.shape[0], table.shape[1]
    patches = total.shape[0] // n_narrow
    for b in range(n_narrow):
        pltpu.make_async_copy(table.at[b * (patches + 1) + patches], flags.at[b], marks.at[b]).start()
    for b in range(n_narrow + 1):
        count[b] = 0

    def file(w, carry):
        for j in range(ROOM):
            name = names[w * ROOM + j]
            held = jnp.maximum(name, 0)
            b = held // patches
            patch = held - b * patches
            pltpu.make_async_copy(
                table.at[b * (patches + 1) + patch],
                answer.at[w, pl.ds(j * columns, columns)],
                picks,
            ).start()
            chosen = jnp.where(name >= 0, b, n_narrow)
            k = count[chosen]
            count[chosen] = k + 1
            lists[chosen, k] = (((w << SHIFT) | j) << 8) | patch
        return carry

    lax.fori_loop(0, n_wide, file, 0)
    scale[...] = jnp.exp2(arrived[:, ROOM * columns :, :].astype(jnp.int32).astype(jnp.float32) * (1.0 / STEPS)) * (1.0 / TOP)

    def leave(b, at):
        return pltpu.make_async_copy(acc.at[at], total.at[pl.ds(b * patches, patches)], outs.at[at])

    for b in range(n_narrow):
        at = b % 2
        if b >= 2:
            leave(b - 2, at).wait()
        acc[at] = jnp.zeros(acc.shape[1:], jnp.float32)

        def add(k, carry):
            entry = lists[b, k]
            patch = entry & 255
            place = (entry >> 8) & ((1 << SHIFT) - 1)
            w = entry >> (8 + SHIFT)
            value = arrived[w, pl.ds(pl.multiple_of(place * columns, 16), columns), :].astype(jnp.int32).astype(jnp.float32)
            acc[at, patch] += value * scale[w, pl.ds(place, 1), :]
            return carry

        lax.fori_loop(0, count[b], add, 0)
        leave(b, at).start()
    fullest = None
    for b in range(n_narrow):
        pltpu.make_async_copy(table.at[b * (patches + 1) + patches], flags.at[b], marks.at[b]).wait()
        mine = flags[b, 0:META, :].astype(jnp.float32)
        fullest = mine if fullest is None else jnp.maximum(fullest, mine)
    for w in range(n_wide):
        answer[w, ROOM * columns :, :] = fullest.astype(answer.dtype)
    every = answer.at[:, pl.ds(0, ROOM * columns)]
    pltpu.make_async_copy(every, every, picks).wait()
    for b in (n_narrow - 2, n_narrow - 1):
        leave(b, b % 2).wait()


def face_kernel(fpatch, slot, arrived, tiles, face, over, buf, sems):
    columns = face.shape[1]
    face[...] = jnp.zeros_like(face)

    def body(p, tile):
        w = slot[p] >> SHIFT
        place = slot[p] & ((1 << SHIFT) - 1)
        moved = arrived[w, pl.ds(pl.multiple_of(place * columns, 16), columns), :]
        face[fpatch[p]] += lax.dot_general(
            moved, tile[...], (((1,), (1,)), ((), ())), preferred_element_type=jnp.float32
        )

    stream_tiles(tiles, buf, sems, body)
    over[0] = jnp.max(arrived[:, ROOM * columns :, :].astype(jnp.float32)).astype(jnp.int32)


def shards(disp, loads, tiles, pair_fpatch, pair_sdev, pair_spatch):
    n_wide = lax.axis_size("wide")
    n_narrow = lax.axis_size("narrow")
    pairs, faces, nodes = tiles.shape
    patches, columns, _ = disp.shape
    rows = ROOM * columns + META
    sdev = pair_sdev[:, 0]
    vmem = pl.BlockSpec(memory_space=pltpu.VMEM)
    smem = pl.BlockSpec(memory_space=pltpu.SMEM)
    hbm = pl.BlockSpec(memory_space=pl.ANY)
    limit = pltpu.CompilerParams(vmem_limit_bytes=24 << 20)
    tile_buf = pltpu.VMEM((DEPTH, GROUP, faces, nodes), tiles.dtype)
    tile_sems = pltpu.SemaphoreType.DMA((DEPTH,))
    flops = 2 * pairs * columns * faces * nodes
    out, slot, aug = pl.pallas_call(
        functools.partial(send_kernel, n_narrow),
        out_shape=(
            jax.ShapeDtypeStruct((n_wide, rows, nodes), jnp.int16),
            jax.ShapeDtypeStruct((pairs,), jnp.int32),
            jax.ShapeDtypeStruct((patches + 1, columns, nodes), disp.dtype),
        ),
        in_specs=[smem, smem, smem, vmem, hbm, hbm],
        out_specs=(vmem, smem, hbm),
        scratch_shapes=[
            tile_buf,
            pltpu.VMEM((n_wide, META, nodes), jnp.int32),
            pltpu.VMEM((1, columns, nodes), disp.dtype),
            pltpu.SMEM((n_wide,), jnp.int32),
            tile_sems,
            pltpu.SemaphoreType.DMA,
        ],
        compiler_params=limit,
        cost_estimate=pl.CostEstimate(flops=flops, bytes_accessed=2 * tiles.size, transcendentals=0),
        name="send",
    )(pair_fpatch, sdev, pair_spatch, loads, tiles, disp)
    table = lax.all_gather(aug, "narrow", axis=0, tiled=True)
    arrived = lax.all_to_all(out, "wide", split_axis=0, concat_axis=0, tiled=True)
    names = arrived[:, ROOM * columns + ROOM, :ROOM].astype(jnp.int32).reshape(n_wide * ROOM)
    total, answer = pl.pallas_call(
        functools.partial(turn_kernel, n_narrow),
        out_shape=(
            jax.ShapeDtypeStruct((n_narrow * patches, columns, nodes), jnp.float32),
            jax.ShapeDtypeStruct((n_wide, rows, nodes), disp.dtype),
        ),
        in_specs=[smem, vmem, hbm],
        out_specs=(hbm, vmem),
        scratch_shapes=[
            pltpu.VMEM((2, patches, columns, nodes), jnp.float32),
            pltpu.VMEM((n_wide, META, nodes), jnp.float32),
            pltpu.VMEM((n_narrow, columns, nodes), disp.dtype),
            pltpu.SMEM((n_narrow + 1, n_wide * ROOM), jnp.int32),
            pltpu.SMEM((n_narrow + 1,), jnp.int32),
            pltpu.SemaphoreType.DMA,
            pltpu.SemaphoreType.DMA((n_narrow,)),
            pltpu.SemaphoreType.DMA((2,)),
        ],
        compiler_params=limit,
        cost_estimate=pl.CostEstimate(flops=10**7, bytes_accessed=2 * 10**7, transcendentals=0),
        name="turn",
    )(names, arrived, table)
    struct_loads = lax.psum_scatter(total, "narrow", scatter_dimension=0, tiled=True)
    back = lax.all_to_all(answer, "wide", split_axis=0, concat_axis=0, tiled=True)
    face_disp, over = pl.pallas_call(
        face_kernel,
        out_shape=(
            jax.ShapeDtypeStruct((loads.shape[0], columns, faces), jnp.float32),
            jax.ShapeDtypeStruct((1,), jnp.int32),
        ),
        in_specs=[smem, smem, vmem, hbm],
        out_specs=(vmem, smem),
        scratch_shapes=[tile_buf, tile_sems],
        compiler_params=limit,
        cost_estimate=pl.CostEstimate(flops=flops, bytes_accessed=2 * tiles.size, transcendentals=0),
        name="face",
    )(pair_fpatch, slot, back, tiles)
    return lax.cond(
        over[0] > ROOM,
        lambda f, s: long_way(disp, loads, tiles, pair_fpatch, sdev, pair_spatch),
        lambda f, s: (f, s),
        face_disp,
        struct_loads,
    )


def solution(mesh):
    placed = (
        P(("wide", "narrow"), None, None),
        P(("wide", "narrow"), None, None),
        P(("wide", "narrow"), None, None),
        P(("wide", "narrow")),
        P(("wide", "narrow"), None),
        P(("wide", "narrow")),
    )
    return jax.shard_map(
        shards,
        mesh=mesh,
        in_specs=placed,
        out_specs=(P(("wide", "narrow"), None, None), P(("wide", "narrow"), None, None)),
        check_vma=False,
    )
```

```python
import functools

import jax
import jax.numpy as jnp
from jax import lax
from jax.experimental import pallas as pl
from jax.experimental.pallas import tpu as pltpu
from jax.sharding import PartitionSpec as P

ROOM = 12
META = 16
SHIFT = 4
GROUP = 16
STEPS = 128.0
TOP = 32760.0
LIMIT = 63 << 20


def long_way(disp, loads, tiles, pair_fpatch, pair_sdev, pair_spatch):
    n_wide = lax.axis_size("wide")
    n_narrow = lax.axis_size("narrow")
    n_dev = n_wide * n_narrow
    pair_count = tiles.shape[0]
    capacity = max(2, 2 * pair_count // n_dev)
    slot_count = n_dev * capacity
    columns = disp.shape[1]
    node_count = disp.shape[2]
    face_count = loads.shape[2]
    target = pair_sdev
    same_target = target[:, None] == target[None, :]
    earlier = lax.broadcasted_iota(jnp.int32, (pair_count, pair_count), 0) > lax.broadcasted_iota(
        jnp.int32, (pair_count, pair_count), 1
    )
    place = jnp.sum((same_target & earlier).astype(jnp.int32), axis=1)
    slot_of_pair = target * capacity + place
    hits = slot_of_pair[None, :] == jnp.arange(slot_count, dtype=jnp.int32)[:, None]
    filled = jnp.any(hits, axis=1)
    pair_of_slot = jnp.sum(
        jnp.where(hits, jnp.arange(pair_count, dtype=jnp.int32)[None, :], 0), axis=1
    )
    request = jnp.where(filled, pair_spatch[pair_of_slot], -1).reshape(n_dev, capacity)
    asked = lax.all_to_all(request, ("wide", "narrow"), split_axis=0, concat_axis=0, tiled=True)
    wanted = asked >= 0
    picked = disp[jnp.maximum(asked, 0)]
    answer = jnp.where(wanted[:, :, None, None], picked, jnp.zeros_like(picked))
    arrived = lax.all_to_all(answer, ("wide", "narrow"), split_axis=0, concat_axis=0, tiled=True)
    arrived = arrived.reshape(slot_count, columns, node_count)
    moved = arrived[slot_of_pair]
    face_part = jnp.einsum("pcn,pfn->pcf", moved, tiles, preferred_element_type=jnp.float32)
    fluid_onehot = (
        pair_fpatch[None, :] == jnp.arange(loads.shape[0], dtype=jnp.int32)[:, None]
    ).astype(jnp.float32)
    face_disp = jnp.dot(
        fluid_onehot,
        face_part.reshape(pair_count, -1),
        precision=lax.Precision.HIGHEST,
        preferred_element_type=jnp.float32,
    ).reshape(loads.shape[0], columns, face_count)
    pulled = loads[pair_fpatch]
    load_part = jnp.einsum("pcf,pfn->pcn", pulled, tiles, preferred_element_type=jnp.float32)
    outgoing = jnp.where(filled[:, None, None], load_part[pair_of_slot], 0.0).reshape(
        n_dev, capacity, columns, node_count
    )
    returned = lax.all_to_all(outgoing, ("wide", "narrow"), split_axis=0, concat_axis=0, tiled=True)
    returned = returned.reshape(slot_count, columns * node_count)
    struct_onehot = (
        asked.reshape(-1)[None, :] == jnp.arange(disp.shape[0], dtype=jnp.int32)[:, None]
    ).astype(jnp.float32)
    struct_loads = jnp.dot(
        struct_onehot, returned, precision=lax.Precision.HIGHEST, preferred_element_type=jnp.float32
    ).reshape(disp.shape[0], columns, node_count)
    return (face_disp, struct_loads)


def stream(groups, arrive, first, second):
    arrive(0)
    first(0)

    def step(g, carry):
        arrive(g)
        first(g)
        second(g - 1)
        return carry

    lax.fori_loop(1, groups, step, 0)
    second(groups - 1)


def send_kernel(
    n_narrow, fpatch, sdev, spatch, loads, tiles, disp, out, slot, aug,
    buf, parts, most, power, whole, meta, ends, own, count, sems, side, leaving,
):
    n_wide, patches, columns = out.shape[0], disp.shape[0], disp.shape[1]
    groups = tiles.shape[0] // GROUP
    groups = tiles.shape[0] // GROUP

    def tile_copy(g):
        part = pl.ds(g * GROUP, GROUP)
        return pltpu.make_async_copy(tiles.at[part], buf.at[part], sems.at[g])

    for g in range(groups):
        tile_copy(g).start()
    keep = pltpu.make_async_copy(disp, own.at[pl.ds(0, patches)], side.at[0])
    keep.start()
    meta[...] = jnp.zeros_like(meta)
    for w in range(n_wide):
        count[w] = 0
        meta[w, ROOM : ROOM + 1, :] = jnp.full((1, meta.shape[2]), -1, jnp.int32)
    lane = lax.broadcasted_iota(jnp.int32, (1, meta.shape[2]), 1)

    def first(g):
        at = lax.rem(g, 2)
        for i in range(GROUP):
            p = g * GROUP + i
            part = jnp.dot(loads[fpatch[p]], buf[p], preferred_element_type=jnp.float32)
            parts[at, i] = part
            most[at, i : i + 1, :] = jnp.max(jnp.abs(part), axis=0, keepdims=True)

    def second(g):
        at = lax.rem(g, 2)
        steps = jnp.ceil(jnp.log2(jnp.maximum(most[at], 1e-33)) * STEPS)
        unit = TOP * jnp.exp2(steps * (-1.0 / STEPS))
        power[...] = steps.astype(jnp.int32)
        for i in range(GROUP):
            p = g * GROUP + i
            target = sdev[p]
            w = lax.div(target, n_narrow)
            asked = lax.rem(target, n_narrow) * patches + spatch[p]
            seen = count[w]
            count[w] = seen + 1
            place = jnp.minimum(seen, ROOM - 1)
            slot[p] = (w << SHIFT) | place
            rounded = jnp.round(parts[at, i] * unit[i : i + 1, :]).astype(jnp.int32)
            whole[p] = rounded.astype(jnp.int16)
            pltpu.make_async_copy(
                whole.at[p], out.at[w, pl.ds(pl.multiple_of(place * columns, 16), columns)], leaving
            ).start()
            meta[w, pl.ds(place, 1), :] = power[i : i + 1, :]
            names = meta[w, ROOM : ROOM + 1, :]
            meta[w, ROOM : ROOM + 1, :] = jnp.where(lane == place, asked, names)

    stream(groups, lambda g: tile_copy(g).wait(), first, second)
    ends[...] = meta[...].astype(jnp.int16)
    tail = pltpu.make_async_copy(ends, out.at[:, pl.ds(ROOM * columns, META)], side.at[1])
    tail.start()
    fullest = count[0]
    for w in range(1, n_wide):
        fullest = jnp.maximum(fullest, count[w])
    own[patches] = jnp.full(own.shape[1:], fullest.astype(jnp.float32), jnp.float32).astype(own.dtype)
    keep.wait()
    mark = pltpu.make_async_copy(own, aug, side.at[2])
    mark.start()
    pltpu.make_async_copy(whole, whole, leaving).wait()
    tail.wait()
    mark.wait()


def pick_kernel(n_narrow, arrived, table, answer, names, held, gone, meta, wide_names, coming, outs, side):
    n_wide, columns = arrived.shape[0], table.shape[1]
    stride = table.shape[0] // n_narrow
    patches = stride - 1
    ends = pltpu.make_async_copy(arrived.at[:, pl.ds(ROOM * columns, META)], meta, side)
    ends.start()
    loading = [
        pltpu.make_async_copy(
            table.at[pl.ds(b * stride, stride)], held.at[pl.ds(b * stride, stride)], coming.at[b]
        )
        for b in range(n_narrow)
    ]
    for each in loading:
        each.start()
    ends.wait()
    wide_names[...] = meta[...].astype(jnp.int32)[:, ROOM, : wide_names.shape[1]]
    naming = pltpu.make_async_copy(wide_names, names, side)
    naming.start()
    for each in loading:
        each.wait()
    fullest = held[patches, 0:META, :].astype(jnp.float32)
    for b in range(1, n_narrow):
        fullest = jnp.maximum(fullest, held[b * stride + patches, 0:META, :].astype(jnp.float32))
    gone[:, ROOM * columns :, :] = jnp.broadcast_to(fullest, (n_wide,) + fullest.shape).astype(gone.dtype)
    naming.wait()

    def leave(w):
        return pltpu.make_async_copy(gone.at[w], answer.at[w], outs.at[w])

    def send(w, carry):
        for j in range(ROOM):
            name = jnp.maximum(names[w, j], 0)
            gone[w, j * columns : (j + 1) * columns, :] = held[name + lax.div(name, patches)]
        leave(w).start()
        return carry

    lax.fori_loop(0, n_wide, send, 0)
    for w in range(n_wide):
        leave(w).wait()


def total_kernel(n_narrow, names, arrived, total, came, acc, scale, lists, count, coming, outs):
    n_wide, columns = arrived.shape[0], total.shape[1]
    patches = total.shape[0] // n_narrow
    quarter = n_wide // 4
    loading = [
        pltpu.make_async_copy(
            arrived.at[pl.ds(i * quarter, quarter)], came.at[pl.ds(i * quarter, quarter)], coming.at[i]
        )
        for i in range(4)
    ]
    for each in loading:
        each.start()
    for b in range(n_narrow + 1):
        count[b] = 0

    def file(w, carry):
        for j in range(ROOM):
            name = names[w, j]
            held = jnp.maximum(name, 0)
            b = lax.div(held, patches)
            chosen = jnp.where(name >= 0, b, n_narrow)
            k = count[chosen]
            count[chosen] = k + 1
            lists[chosen, k] = (w << 16) | (j << 12) | (j << 8) | (held - b * patches)
        return carry

    lax.fori_loop(0, n_wide, file, 0)
    for b in range(n_narrow):
        lists[b, count[b]] = (META - 1) << 8
    acc[...] = jnp.zeros_like(acc)
    for each in loading:
        each.wait()
    scale[...] = jnp.exp2(came[:, ROOM * columns :, :].astype(jnp.int32).astype(jnp.float32) * (1.0 / STEPS)) * (1.0 / TOP)
    scale[0, META - 1 : META, :] = jnp.zeros((1, scale.shape[2]), jnp.float32)

    def leave(b):
        return pltpu.make_async_copy(acc.at[b % 4], total.at[pl.ds(b * patches, patches)], outs.at[b % 4])

    for b in range(n_narrow):
        at = b % 4
        if b >= 4:
            leave(b - 4).wait()
            acc[at] = jnp.zeros(acc.shape[1:], jnp.float32)

        def add(k, carry):
            terms = []
            for i in range(2):
                entry = lists[b, 2 * k + i]
                patch = entry & 255
                row = (entry >> 8) & 15
                place = (entry >> 12) & 15
                w = entry >> 16
                value = came[w, pl.ds(pl.multiple_of(place * columns, 16), columns), :].astype(jnp.int32).astype(jnp.float32)
                terms.append((patch, value * scale[w, pl.ds(row, 1), :]))
            for patch, term in terms:
                acc[at, patch] += term
            return carry

        lax.fori_loop(0, lax.div(count[b] + 1, 2), add, 0)
        leave(b).start()
    for b in range(n_narrow - 4, n_narrow):
        leave(b).wait()


def face_kernel(fpatch, slot, arrived, tiles, face, over, buf, moved, parts, acc, ends, sems, moves, side):
    columns = face.shape[1]
    groups = tiles.shape[0] // GROUP

    def tile_copy(g):
        part = pl.ds(g * GROUP, GROUP)
        return pltpu.make_async_copy(tiles.at[part], buf.at[part], sems.at[g])

    def pick(g):
        for i in range(GROUP):
            spot = slot[g * GROUP + i]
            place = spot & ((1 << SHIFT) - 1)
            pltpu.make_async_copy(
                arrived.at[spot >> SHIFT, pl.ds(pl.multiple_of(place * columns, 16), columns)],
                moved.at[g * GROUP + i],
                moves.at[g],
            ).start()

    for g in range(groups):
        pick(g)
        tile_copy(g).start()
    tail = pltpu.make_async_copy(arrived.at[:, pl.ds(ROOM * columns, META)], ends, side.at[0])
    tail.start()

    def arrive(g):
        held = moved.at[pl.ds(g * GROUP, GROUP)]
        pltpu.make_async_copy(held, held, moves.at[g]).wait()
        tile_copy(g).wait()

    def first(g):
        at = lax.rem(g, 2)
        for i in range(GROUP):
            p = g * GROUP + i
            parts[at, i] = lax.dot_general(
                moved[p], buf[p], (((1,), (1,)), ((), ())), preferred_element_type=jnp.float32
            )

    def second(g):
        at = lax.rem(g, 2)
        for i in range(GROUP):
            acc[fpatch[g * GROUP + i]] += parts[at, i]

    acc[...] = jnp.zeros_like(acc)
    stream(groups, arrive, first, second)
    out = pltpu.make_async_copy(acc, face, side.at[1])
    out.start()
    tail.wait()
    over[0] = jnp.max(ends[...].astype(jnp.float32)).astype(jnp.int32)
    out.wait()


def shards(disp, loads, tiles, pair_fpatch, pair_sdev, pair_spatch):
    n_wide = lax.axis_size("wide")
    n_narrow = lax.axis_size("narrow")
    pairs, faces, nodes = tiles.shape
    patches, columns, _ = disp.shape
    rows = ROOM * columns + META
    sdev = pair_sdev[:, 0]
    vmem = pl.BlockSpec(memory_space=pltpu.VMEM)
    smem = pl.BlockSpec(memory_space=pltpu.SMEM)
    hbm = pl.BlockSpec(memory_space=pltpu.HBM)
    tile_buf = pltpu.VMEM(tiles.shape, tiles.dtype)
    groups = pairs // GROUP
    part_buf = pltpu.VMEM((2, GROUP, columns, nodes), jnp.float32)
    dma = pltpu.SemaphoreType.DMA
    flops = 2 * pairs * columns * faces * nodes
    out, slot, aug = pl.pallas_call(
        functools.partial(send_kernel, n_narrow),
        out_shape=(
            jax.ShapeDtypeStruct((n_wide, rows, nodes), jnp.int16),
            jax.ShapeDtypeStruct((pairs,), jnp.int32),
            jax.ShapeDtypeStruct((patches + 1, columns, nodes), disp.dtype),
        ),
        in_specs=[smem, smem, smem, vmem, hbm, hbm],
        out_specs=(hbm, smem, hbm),
        scratch_shapes=[
            tile_buf,
            part_buf,
            pltpu.VMEM((2, GROUP, nodes), jnp.float32),
            pltpu.VMEM((GROUP, nodes), jnp.int32),
            pltpu.VMEM((pairs, columns, nodes), jnp.int16),
            pltpu.VMEM((n_wide, META, nodes), jnp.int32),
            pltpu.VMEM((n_wide, META, nodes), jnp.int16),
            pltpu.VMEM((patches + 1, columns, nodes), disp.dtype),
            pltpu.SMEM((n_wide,), jnp.int32),
            dma((groups,)),
            dma((3,)),
            dma,
        ],
        compiler_params=pltpu.CompilerParams(vmem_limit_bytes=LIMIT),
        cost_estimate=pl.CostEstimate(flops=flops, bytes_accessed=2 * tiles.size, transcendentals=0),
        name="send",
    )(pair_fpatch, sdev, pair_spatch, loads, tiles, disp)
    table = lax.all_gather(aug, "narrow", axis=0, tiled=True)
    arrived = lax.all_to_all(out, "wide", split_axis=0, concat_axis=0, tiled=True)
    answer, names = pl.pallas_call(
        functools.partial(pick_kernel, n_narrow),
        out_shape=(
            jax.ShapeDtypeStruct((n_wide, rows, nodes), disp.dtype),
            jax.ShapeDtypeStruct((n_wide, 128), jnp.int32),
        ),
        in_specs=[hbm, hbm],
        out_specs=(hbm, smem),
        scratch_shapes=[
            pltpu.VMEM((n_narrow * (patches + 1), columns, nodes), disp.dtype),
            pltpu.VMEM((n_wide, rows, nodes), disp.dtype),
            pltpu.VMEM((n_wide, META, nodes), jnp.int16),
            pltpu.VMEM((n_wide, 128), jnp.int32),
            dma((n_narrow,)),
            dma((n_wide,)),
            dma,
        ],
        compiler_params=pltpu.CompilerParams(vmem_limit_bytes=LIMIT),
        cost_estimate=pl.CostEstimate(flops=10**6, bytes_accessed=12 * 10**6, transcendentals=0),
        name="pick",
    )(arrived, table)
    back = lax.all_to_all(answer, "wide", split_axis=0, concat_axis=0, tiled=True)
    total = pl.pallas_call(
        functools.partial(total_kernel, n_narrow),
        out_shape=jax.ShapeDtypeStruct((n_narrow * patches, columns, nodes), jnp.float32),
        in_specs=[smem, hbm],
        out_specs=hbm,
        scratch_shapes=[
            pltpu.VMEM((n_wide, rows, nodes), jnp.int16),
            pltpu.VMEM((4, patches, columns, nodes), jnp.float32),
            pltpu.VMEM((n_wide, META, nodes), jnp.float32),
            pltpu.SMEM((n_narrow + 1, n_wide * ROOM + 1), jnp.int32),
            pltpu.SMEM((n_narrow + 1,), jnp.int32),
            dma((4,)),
            dma((4,)),
        ],
        compiler_params=pltpu.CompilerParams(vmem_limit_bytes=LIMIT),
        cost_estimate=pl.CostEstimate(flops=10**7, bytes_accessed=18 * 10**6, transcendentals=0),
        name="total",
    )(names, arrived)
    struct_loads = lax.psum_scatter(total, "narrow", scatter_dimension=0, tiled=True)
    face_disp, over = pl.pallas_call(
        face_kernel,
        out_shape=(
            jax.ShapeDtypeStruct((loads.shape[0], columns, faces), jnp.float32),
            jax.ShapeDtypeStruct((1,), jnp.int32),
        ),
        in_specs=[smem, smem, hbm, hbm],
        out_specs=(hbm, smem),
        scratch_shapes=[
            tile_buf,
            pltpu.VMEM((pairs, columns, nodes), disp.dtype),
            part_buf,
            pltpu.VMEM((loads.shape[0], columns, faces), jnp.float32),
            pltpu.VMEM((n_wide, META, nodes), disp.dtype),
            dma((groups,)),
            dma((groups,)),
            dma((2,)),
        ],
        compiler_params=pltpu.CompilerParams(vmem_limit_bytes=LIMIT),
        cost_estimate=pl.CostEstimate(flops=flops, bytes_accessed=2 * tiles.size, transcendentals=0),
        name="face",
    )(pair_fpatch, slot, back, tiles)
    return lax.cond(
        over[0] > ROOM,
        lambda f, s: long_way(disp, loads, tiles, pair_fpatch, sdev, pair_spatch),
        lambda f, s: (f, s),
        face_disp,
        struct_loads,
    )


def solution(mesh):
    placed = (
        P(("wide", "narrow"), None, None),
        P(("wide", "narrow"), None, None),
        P(("wide", "narrow"), None, None),
        P(("wide", "narrow")),
        P(("wide", "narrow"), None),
        P(("wide", "narrow")),
    )
    return jax.shard_map(
        shards,
        mesh=mesh,
        in_specs=placed,
        out_specs=(P(("wide", "narrow"), None, None), P(("wide", "narrow"), None, None)),
        check_vma=False,
    )
```

```python
import functools

import jax
import jax.numpy as jnp
from jax import lax
from jax.experimental import pallas as pl
from jax.experimental.pallas import tpu as pltpu
from jax.sharding import PartitionSpec as P

ROOM = 12
META = 16
SHIFT = 4
GROUP = 16
AHEAD = 4
STEPS = 128.0
TOP = 32760.0
LIMIT = 63 << 20


def long_way(disp, loads, tiles, pair_fpatch, pair_sdev, pair_spatch):
    n_wide = lax.axis_size("wide")
    n_narrow = lax.axis_size("narrow")
    n_dev = n_wide * n_narrow
    pair_count = tiles.shape[0]
    capacity = max(2, 2 * pair_count // n_dev)
    slot_count = n_dev * capacity
    columns = disp.shape[1]
    node_count = disp.shape[2]
    face_count = loads.shape[2]
    target = pair_sdev
    same_target = target[:, None] == target[None, :]
    earlier = lax.broadcasted_iota(jnp.int32, (pair_count, pair_count), 0) > lax.broadcasted_iota(
        jnp.int32, (pair_count, pair_count), 1
    )
    place = jnp.sum((same_target & earlier).astype(jnp.int32), axis=1)
    slot_of_pair = target * capacity + place
    hits = slot_of_pair[None, :] == jnp.arange(slot_count, dtype=jnp.int32)[:, None]
    filled = jnp.any(hits, axis=1)
    pair_of_slot = jnp.sum(
        jnp.where(hits, jnp.arange(pair_count, dtype=jnp.int32)[None, :], 0), axis=1
    )
    request = jnp.where(filled, pair_spatch[pair_of_slot], -1).reshape(n_dev, capacity)
    asked = lax.all_to_all(request, ("wide", "narrow"), split_axis=0, concat_axis=0, tiled=True)
    wanted = asked >= 0
    picked = disp[jnp.maximum(asked, 0)]
    answer = jnp.where(wanted[:, :, None, None], picked, jnp.zeros_like(picked))
    arrived = lax.all_to_all(answer, ("wide", "narrow"), split_axis=0, concat_axis=0, tiled=True)
    arrived = arrived.reshape(slot_count, columns, node_count)
    moved = arrived[slot_of_pair]
    face_part = jnp.einsum("pcn,pfn->pcf", moved, tiles, preferred_element_type=jnp.float32)
    fluid_onehot = (
        pair_fpatch[None, :] == jnp.arange(loads.shape[0], dtype=jnp.int32)[:, None]
    ).astype(jnp.float32)
    face_disp = jnp.dot(
        fluid_onehot,
        face_part.reshape(pair_count, -1),
        precision=lax.Precision.HIGHEST,
        preferred_element_type=jnp.float32,
    ).reshape(loads.shape[0], columns, face_count)
    pulled = loads[pair_fpatch]
    load_part = jnp.einsum("pcf,pfn->pcn", pulled, tiles, preferred_element_type=jnp.float32)
    outgoing = jnp.where(filled[:, None, None], load_part[pair_of_slot], 0.0).reshape(
        n_dev, capacity, columns, node_count
    )
    returned = lax.all_to_all(outgoing, ("wide", "narrow"), split_axis=0, concat_axis=0, tiled=True)
    returned = returned.reshape(slot_count, columns * node_count)
    struct_onehot = (
        asked.reshape(-1)[None, :] == jnp.arange(disp.shape[0], dtype=jnp.int32)[:, None]
    ).astype(jnp.float32)
    struct_loads = jnp.dot(
        struct_onehot, returned, precision=lax.Precision.HIGHEST, preferred_element_type=jnp.float32
    ).reshape(disp.shape[0], columns, node_count)
    return (face_disp, struct_loads)


def tile_copy(tiles, buf, sems, g):
    part = pl.ds(g * GROUP, GROUP)
    return pltpu.make_async_copy(tiles.at[part], buf.at[part], sems.at[g])


def send_kernel(
    n_narrow, fpatch, sdev, spatch, loads, tiles, disp, out, slot, aug,
    buf, parts, most, power, whole, meta, ends, own, count, sems, side, leaving,
):
    n_wide, patches, columns = out.shape[0], disp.shape[0], disp.shape[1]
    groups = tiles.shape[0] // GROUP
    groups = tiles.shape[0] // GROUP

    for g in range(groups):
        tile_copy(tiles, buf, sems, g).start()
    keep = pltpu.make_async_copy(disp, own.at[pl.ds(0, patches)], side.at[0])
    keep.start()
    meta[...] = jnp.zeros_like(meta)
    for w in range(n_wide):
        count[w] = 0
        meta[w, ROOM : ROOM + 1, :] = jnp.full((1, meta.shape[2]), -1, jnp.int32)
    lane = lax.broadcasted_iota(jnp.int32, (1, meta.shape[2]), 1)

    def first(g):
        at = lax.rem(g, 2)
        for i in range(GROUP):
            p = g * GROUP + i
            part = jnp.dot(loads[fpatch[p]], buf[p], preferred_element_type=jnp.float32)
            parts[at, i] = part
            most[at, i : i + 1, :] = jnp.max(jnp.abs(part), axis=0, keepdims=True)

    def second(g):
        at = lax.rem(g, 2)
        steps = jnp.ceil(jnp.log2(jnp.maximum(most[at], 1e-33)) * STEPS)
        unit = TOP * jnp.exp2(steps * (-1.0 / STEPS))
        power[...] = steps.astype(jnp.int32)
        for i in range(GROUP):
            p = g * GROUP + i
            target = sdev[p]
            w = lax.div(target, n_narrow)
            asked = lax.rem(target, n_narrow) * patches + spatch[p]
            seen = count[w]
            count[w] = seen + 1
            place = jnp.minimum(seen, ROOM - 1)
            slot[p] = (w << SHIFT) | place
            rounded = jnp.round(parts[at, i] * unit[i : i + 1, :]).astype(jnp.int32)
            whole[p] = rounded.astype(jnp.int16)
            pltpu.make_async_copy(
                whole.at[p], out.at[w, pl.ds(pl.multiple_of(place * columns, 16), columns)], leaving
            ).start()
            meta[w, pl.ds(place, 1), :] = power[i : i + 1, :]
            names = meta[w, ROOM : ROOM + 1, :]
            meta[w, ROOM : ROOM + 1, :] = jnp.where(lane == place, asked, names)


    tile_copy(tiles, buf, sems, 0).wait()
    first(0)

    def step(g, carry):
        tile_copy(tiles, buf, sems, g).wait()
        first(g)
        second(g - 1)
        return carry

    lax.fori_loop(1, groups, step, 0)
    second(groups - 1)
    ends[...] = meta[...].astype(jnp.int16)
    tail = pltpu.make_async_copy(ends, out.at[:, pl.ds(ROOM * columns, META)], side.at[1])
    tail.start()
    fullest = count[0]
    for w in range(1, n_wide):
        fullest = jnp.maximum(fullest, count[w])
    own[patches] = jnp.full(own.shape[1:], fullest.astype(jnp.float32), jnp.float32).astype(own.dtype)
    keep.wait()
    mark = pltpu.make_async_copy(own, aug, side.at[2])
    mark.start()
    pltpu.make_async_copy(whole, whole, leaving).wait()
    tail.wait()
    mark.wait()


def turn_kernel(
    n_narrow, arrived, table, total, answer,
    held, gone, came, acc, scale, meta, wide_names, names, lists, count, tables, comes, goes, outs, side,
):
    n_wide, columns = arrived.shape[0], table.shape[1]
    stride = table.shape[0] // n_narrow
    patches = stride - 1
    quarter = n_wide // 4
    ends = pltpu.make_async_copy(arrived.at[:, pl.ds(ROOM * columns, META)], meta, side)
    ends.start()
    loading = [
        pltpu.make_async_copy(
            table.at[pl.ds(b * stride, stride)], held.at[pl.ds(b * stride, stride)], tables.at[b]
        )
        for b in range(n_narrow)
    ]
    coming = [
        pltpu.make_async_copy(
            arrived.at[pl.ds(i * quarter, quarter)], came.at[pl.ds(i * quarter, quarter)], comes.at[i]
        )
        for i in range(4)
    ]
    for each in loading + coming:
        each.start()
    for b in range(n_narrow + 1):
        count[b] = 0
    ends.wait()
    wide_names[...] = meta[...].astype(jnp.int32)[:, ROOM, : wide_names.shape[1]]
    naming = pltpu.make_async_copy(wide_names, names, side)
    naming.start()
    scale[...] = jnp.exp2(meta[...].astype(jnp.int32).astype(jnp.float32) * (1.0 / STEPS)) * (1.0 / TOP)
    scale[0, META - 1 : META, :] = jnp.zeros((1, scale.shape[2]), jnp.float32)
    acc[...] = jnp.zeros_like(acc)
    for each in loading:
        each.wait()
    fullest = held[patches, 0:META, :].astype(jnp.float32)
    for b in range(1, n_narrow):
        fullest = jnp.maximum(fullest, held[b * stride + patches, 0:META, :].astype(jnp.float32))
    gone[:, ROOM * columns :, :] = jnp.broadcast_to(fullest, (n_wide,) + fullest.shape).astype(gone.dtype)
    naming.wait()

    def away(w):
        return pltpu.make_async_copy(gone.at[w], answer.at[w], goes.at[w])

    def send(w, carry):
        for j in range(ROOM):
            name = names[w, j]
            asked = jnp.maximum(name, 0)
            b = lax.div(asked, patches)
            gone[w, j * columns : (j + 1) * columns, :] = held[asked + b]
            chosen = jnp.where(name >= 0, b, n_narrow)
            k = count[chosen]
            count[chosen] = k + 1
            lists[chosen, k] = (w << 16) | (j << 12) | (j << 8) | (asked - b * patches)
        away(w).start()
        return carry

    lax.fori_loop(0, n_wide, send, 0)
    for b in range(n_narrow):
        lists[b, count[b]] = (META - 1) << 8
    for each in coming:
        each.wait()

    def leave(b):
        return pltpu.make_async_copy(acc.at[b % 4], total.at[pl.ds(b * patches, patches)], outs.at[b % 4])

    for b in range(n_narrow):
        at = b % 4
        if b >= 4:
            leave(b - 4).wait()
            acc[at] = jnp.zeros(acc.shape[1:], jnp.float32)

        def add(k, carry):
            terms = []
            for i in range(2):
                entry = lists[b, 2 * k + i]
                patch = entry & 255
                row = (entry >> 8) & 15
                place = (entry >> 12) & 15
                w = entry >> 16
                value = came[w, pl.ds(pl.multiple_of(place * columns, 16), columns), :].astype(jnp.int32).astype(jnp.float32)
                terms.append((patch, value * scale[w, pl.ds(row, 1), :]))
            for patch, term in terms:
                acc[at, patch] += term
            return carry

        lax.fori_loop(0, lax.div(count[b] + 1, 2), add, 0)
        leave(b).start()
    for w in range(n_wide):
        away(w).wait()
    for b in range(n_narrow - 4, n_narrow):
        leave(b).wait()


def face_kernel(fpatch, slot, arrived, tiles, face, over, buf, moved, acc, ends, sems, moves, side):
    columns = face.shape[1]
    groups = tiles.shape[0] // GROUP

    def fetch(g):
        for i in range(GROUP):
            spot = slot[g * GROUP + i]
            place = spot & ((1 << SHIFT) - 1)
            pltpu.make_async_copy(
                arrived.at[spot >> SHIFT, pl.ds(pl.multiple_of(place * columns, 16), columns)],
                moved.at[g * GROUP + i],
                moves.at[g],
            ).start()
        tile_copy(tiles, buf, sems, g).start()

    for g in range(AHEAD):
        fetch(g)
    tail = pltpu.make_async_copy(arrived.at[:, pl.ds(ROOM * columns, META)], ends, side.at[0])
    tail.start()
    acc[...] = jnp.zeros_like(acc)

    def step(g, carry):
        held = moved.at[pl.ds(g * GROUP, GROUP)]
        pltpu.make_async_copy(held, held, moves.at[g]).wait()
        tile_copy(tiles, buf, sems, g).wait()

        @pl.when(g + AHEAD < groups)
        def _():
            fetch(g + AHEAD)

        for i in range(GROUP):
            p = g * GROUP + i
            acc[fpatch[p]] += lax.dot_general(
                moved[p], buf[p], (((1,), (1,)), ((), ())), preferred_element_type=jnp.float32
            )
        return carry

    lax.fori_loop(0, groups, step, 0)
    out = pltpu.make_async_copy(acc, face, side.at[1])
    out.start()
    tail.wait()
    over[0] = jnp.max(ends[...].astype(jnp.float32)).astype(jnp.int32)
    out.wait()


def shards(disp, loads, tiles, pair_fpatch, pair_sdev, pair_spatch):
    n_wide = lax.axis_size("wide")
    n_narrow = lax.axis_size("narrow")
    pairs, faces, nodes = tiles.shape
    patches, columns, _ = disp.shape
    rows = ROOM * columns + META
    sdev = pair_sdev[:, 0]
    vmem = pl.BlockSpec(memory_space=pltpu.VMEM)
    smem = pl.BlockSpec(memory_space=pltpu.SMEM)
    hbm = pl.BlockSpec(memory_space=pltpu.HBM)
    tile_buf = pltpu.VMEM(tiles.shape, tiles.dtype)
    groups = pairs // GROUP
    part_buf = pltpu.VMEM((2, GROUP, columns, nodes), jnp.float32)
    dma = pltpu.SemaphoreType.DMA
    flops = 2 * pairs * columns * faces * nodes
    out, slot, aug = pl.pallas_call(
        functools.partial(send_kernel, n_narrow),
        out_shape=(
            jax.ShapeDtypeStruct((n_wide, rows, nodes), jnp.int16),
            jax.ShapeDtypeStruct((pairs,), jnp.int32),
            jax.ShapeDtypeStruct((patches + 1, columns, nodes), disp.dtype),
        ),
        in_specs=[smem, smem, smem, vmem, hbm, hbm],
        out_specs=(hbm, smem, hbm),
        scratch_shapes=[
            tile_buf,
            part_buf,
            pltpu.VMEM((2, GROUP, nodes), jnp.float32),
            pltpu.VMEM((GROUP, nodes), jnp.int32),
            pltpu.VMEM((pairs, columns, nodes), jnp.int16),
            pltpu.VMEM((n_wide, META, nodes), jnp.int32),
            pltpu.VMEM((n_wide, META, nodes), jnp.int16),
            pltpu.VMEM((patches + 1, columns, nodes), disp.dtype),
            pltpu.SMEM((n_wide,), jnp.int32),
            dma((groups,)),
            dma((3,)),
            dma,
        ],
        compiler_params=pltpu.CompilerParams(vmem_limit_bytes=LIMIT),
        cost_estimate=pl.CostEstimate(flops=flops, bytes_accessed=2 * tiles.size, transcendentals=0),
        name="send",
    )(pair_fpatch, sdev, pair_spatch, loads, tiles, disp)
    table = lax.all_gather(aug, "narrow", axis=0, tiled=True)
    arrived = lax.all_to_all(out, "wide", split_axis=0, concat_axis=0, tiled=True)
    total, answer = pl.pallas_call(
        functools.partial(turn_kernel, n_narrow),
        out_shape=(
            jax.ShapeDtypeStruct((n_narrow * patches, columns, nodes), jnp.float32),
            jax.ShapeDtypeStruct((n_wide, rows, nodes), disp.dtype),
        ),
        in_specs=[hbm, hbm],
        out_specs=(hbm, hbm),
        scratch_shapes=[
            pltpu.VMEM((n_narrow * (patches + 1), columns, nodes), disp.dtype),
            pltpu.VMEM((n_wide, rows, nodes), disp.dtype),
            pltpu.VMEM((n_wide, rows, nodes), jnp.int16),
            pltpu.VMEM((4, patches, columns, nodes), jnp.float32),
            pltpu.VMEM((n_wide, META, nodes), jnp.float32),
            pltpu.VMEM((n_wide, META, nodes), jnp.int16),
            pltpu.VMEM((n_wide, 128), jnp.int32),
            pltpu.SMEM((n_wide, 128), jnp.int32),
            pltpu.SMEM((n_narrow + 1, n_wide * ROOM + 1), jnp.int32),
            pltpu.SMEM((n_narrow + 1,), jnp.int32),
            dma((n_narrow,)),
            dma((4,)),
            dma((n_wide,)),
            dma((4,)),
            dma,
        ],
        compiler_params=pltpu.CompilerParams(vmem_limit_bytes=LIMIT),
        cost_estimate=pl.CostEstimate(flops=10**7, bytes_accessed=29 * 10**6, transcendentals=0),
        name="turn",
    )(arrived, table)
    back = lax.all_to_all(answer, "wide", split_axis=0, concat_axis=0, tiled=True)
    struct_loads = lax.psum_scatter(total, "narrow", scatter_dimension=0, tiled=True)
    face_disp, over = pl.pallas_call(
        face_kernel,
        out_shape=(
            jax.ShapeDtypeStruct((loads.shape[0], columns, faces), jnp.float32),
            jax.ShapeDtypeStruct((1,), jnp.int32),
        ),
        in_specs=[smem, smem, hbm, hbm],
        out_specs=(hbm, smem),
        scratch_shapes=[
            tile_buf,
            pltpu.VMEM((pairs, columns, nodes), disp.dtype),
            pltpu.VMEM((loads.shape[0], columns, faces), jnp.float32),
            pltpu.VMEM((n_wide, META, nodes), disp.dtype),
            dma((groups,)),
            dma((groups,)),
            dma((2,)),
        ],
        compiler_params=pltpu.CompilerParams(vmem_limit_bytes=LIMIT),
        cost_estimate=pl.CostEstimate(flops=flops, bytes_accessed=2 * tiles.size, transcendentals=0),
        name="face",
    )(pair_fpatch, slot, back, tiles)
    return lax.cond(
        over[0] > ROOM,
        lambda f, s: long_way(disp, loads, tiles, pair_fpatch, sdev, pair_spatch),
        lambda f, s: (f, s),
        face_disp,
        struct_loads,
    )


def solution(mesh):
    placed = (
        P(("wide", "narrow"), None, None),
        P(("wide", "narrow"), None, None),
        P(("wide", "narrow"), None, None),
        P(("wide", "narrow")),
        P(("wide", "narrow"), None),
        P(("wide", "narrow")),
    )
    return jax.shard_map(
        shards,
        mesh=mesh,
        in_specs=placed,
        out_specs=(P(("wide", "narrow"), None, None), P(("wide", "narrow"), None, None)),
        check_vma=False,
    )
```

```python
import functools

import jax
import jax.numpy as jnp
from jax import lax
from jax.experimental import pallas as pl
from jax.experimental.pallas import tpu as pltpu
from jax.sharding import PartitionSpec as P

ROOM = 12
META = 16
SHIFT = 4
GROUP = 16
AHEAD = 4
STEPS = 128.0
TOP = 32760.0
MARK = 1e37
LIMIT = 63 << 20


def long_way(disp, loads, tiles, pair_fpatch, pair_sdev, pair_spatch):
    n_wide = lax.axis_size("wide")
    n_narrow = lax.axis_size("narrow")
    n_dev = n_wide * n_narrow
    pair_count = tiles.shape[0]
    capacity = max(2, 2 * pair_count // n_dev)
    slot_count = n_dev * capacity
    columns = disp.shape[1]
    node_count = disp.shape[2]
    face_count = loads.shape[2]
    target = pair_sdev
    same_target = target[:, None] == target[None, :]
    earlier = lax.broadcasted_iota(jnp.int32, (pair_count, pair_count), 0) > lax.broadcasted_iota(
        jnp.int32, (pair_count, pair_count), 1
    )
    place = jnp.sum((same_target & earlier).astype(jnp.int32), axis=1)
    slot_of_pair = target * capacity + place
    hits = slot_of_pair[None, :] == jnp.arange(slot_count, dtype=jnp.int32)[:, None]
    filled = jnp.any(hits, axis=1)
    pair_of_slot = jnp.sum(
        jnp.where(hits, jnp.arange(pair_count, dtype=jnp.int32)[None, :], 0), axis=1
    )
    request = jnp.where(filled, pair_spatch[pair_of_slot], -1).reshape(n_dev, capacity)
    asked = lax.all_to_all(request, ("wide", "narrow"), split_axis=0, concat_axis=0, tiled=True)
    wanted = asked >= 0
    picked = disp[jnp.maximum(asked, 0)]
    answer = jnp.where(wanted[:, :, None, None], picked, jnp.zeros_like(picked))
    arrived = lax.all_to_all(answer, ("wide", "narrow"), split_axis=0, concat_axis=0, tiled=True)
    arrived = arrived.reshape(slot_count, columns, node_count)
    moved = arrived[slot_of_pair]
    face_part = jnp.einsum("pcn,pfn->pcf", moved, tiles, preferred_element_type=jnp.float32)
    fluid_onehot = (
        pair_fpatch[None, :] == jnp.arange(loads.shape[0], dtype=jnp.int32)[:, None]
    ).astype(jnp.float32)
    face_disp = jnp.dot(
        fluid_onehot,
        face_part.reshape(pair_count, -1),
        precision=lax.Precision.HIGHEST,
        preferred_element_type=jnp.float32,
    ).reshape(loads.shape[0], columns, face_count)
    pulled = loads[pair_fpatch]
    load_part = jnp.einsum("pcf,pfn->pcn", pulled, tiles, preferred_element_type=jnp.float32)
    outgoing = jnp.where(filled[:, None, None], load_part[pair_of_slot], 0.0).reshape(
        n_dev, capacity, columns, node_count
    )
    returned = lax.all_to_all(outgoing, ("wide", "narrow"), split_axis=0, concat_axis=0, tiled=True)
    returned = returned.reshape(slot_count, columns * node_count)
    struct_onehot = (
        asked.reshape(-1)[None, :] == jnp.arange(disp.shape[0], dtype=jnp.int32)[:, None]
    ).astype(jnp.float32)
    struct_loads = jnp.dot(
        struct_onehot, returned, precision=lax.Precision.HIGHEST, preferred_element_type=jnp.float32
    ).reshape(disp.shape[0], columns, node_count)
    return (face_disp, struct_loads)


def tile_copy(tiles, buf, sems, g):
    part = pl.ds(g * GROUP, GROUP)
    return pltpu.make_async_copy(tiles.at[part], buf.at[part], sems.at[g])


def send_kernel(
    n_narrow, patches, fpatch, sdev, spatch, loads, tiles, out, slot,
    buf, parts, most, power, whole, meta, ends, count, sems, side, leaving,
):
    n_wide, columns = out.shape[0], whole.shape[1]
    groups = tiles.shape[0] // GROUP
    groups = tiles.shape[0] // GROUP

    for g in range(groups):
        tile_copy(tiles, buf, sems, g).start()
    meta[...] = jnp.zeros_like(meta)
    for w in range(n_wide):
        count[w] = 0
        meta[w, ROOM : ROOM + 1, :] = jnp.full((1, meta.shape[2]), -1, jnp.int32)
    lane = lax.broadcasted_iota(jnp.int32, (1, meta.shape[2]), 1)

    def first(g):
        at = lax.rem(g, 2)
        for i in range(GROUP):
            p = g * GROUP + i
            part = jnp.dot(loads[fpatch[p]], buf[p], preferred_element_type=jnp.float32)
            parts[at, i] = part
            most[at, i : i + 1, :] = jnp.max(jnp.abs(part), axis=0, keepdims=True)

    def second(g):
        at = lax.rem(g, 2)
        steps = jnp.ceil(jnp.log2(jnp.maximum(most[at], 1e-33)) * STEPS)
        unit = TOP * jnp.exp2(steps * (-1.0 / STEPS))
        power[...] = steps.astype(jnp.int32)
        for i in range(GROUP):
            p = g * GROUP + i
            target = sdev[p]
            w = lax.div(target, n_narrow)
            asked = lax.rem(target, n_narrow) * patches + spatch[p]
            seen = count[w]
            count[w] = seen + 1
            place = jnp.minimum(seen, ROOM - 1)
            slot[p] = (w << SHIFT) | place
            rounded = jnp.round(parts[at, i] * unit[i : i + 1, :]).astype(jnp.int32)
            whole[p] = rounded.astype(jnp.int16)
            pltpu.make_async_copy(
                whole.at[p], out.at[w, pl.ds(pl.multiple_of(place * columns, 16), columns)], leaving
            ).start()
            meta[w, pl.ds(place, 1), :] = power[i : i + 1, :]
            names = meta[w, ROOM : ROOM + 1, :]
            meta[w, ROOM : ROOM + 1, :] = jnp.where(lane == place, asked, names)


    tile_copy(tiles, buf, sems, 0).wait()
    first(0)

    def step(g, carry):
        tile_copy(tiles, buf, sems, g).wait()
        first(g)
        second(g - 1)
        return carry

    lax.fori_loop(1, groups, step, 0)
    second(groups - 1)
    fullest = count[0]
    for w in range(1, n_wide):
        fullest = jnp.maximum(fullest, count[w])
    for w in range(n_wide):
        names = meta[w, ROOM : ROOM + 1, :]
        meta[w, ROOM : ROOM + 1, :] = jnp.where(lane == ROOM, fullest, names)
    ends[...] = meta[...].astype(jnp.int16)
    tail = pltpu.make_async_copy(ends, out.at[:, pl.ds(ROOM * columns, META)], side)
    tail.start()
    pltpu.make_async_copy(whole, whole, leaving).wait()
    tail.wait()


def turn_kernel(
    n_narrow, arrived, table, total, answer,
    held, gone, came, acc, scale, meta, wide_names, names, lists, count, tables, comes, goes, outs, side,
):
    n_wide, columns = arrived.shape[0], table.shape[1]
    patches = table.shape[0] // n_narrow
    quarter = n_wide // 4
    ends = pltpu.make_async_copy(arrived.at[:, pl.ds(ROOM * columns, META)], meta, side)
    ends.start()
    loading = [
        pltpu.make_async_copy(
            table.at[pl.ds(b * patches, patches)], held.at[pl.ds(b * patches, patches)], tables.at[b]
        )
        for b in range(n_narrow)
    ]
    coming = [
        pltpu.make_async_copy(
            arrived.at[pl.ds(i * quarter, quarter)], came.at[pl.ds(i * quarter, quarter)], comes.at[i]
        )
        for i in range(4)
    ]
    for each in loading + coming:
        each.start()
    for b in range(n_narrow + 1):
        count[b] = 0
    ends.wait()
    wide_names[...] = meta[...].astype(jnp.int32)[:, ROOM, : wide_names.shape[1]]
    naming = pltpu.make_async_copy(wide_names, names, side)
    naming.start()
    scale[...] = jnp.exp2(meta[...].astype(jnp.int32).astype(jnp.float32) * (1.0 / STEPS)) * (1.0 / TOP)
    scale[0, META - 1 : META, :] = jnp.zeros((1, scale.shape[2]), jnp.float32)
    acc[...] = jnp.zeros_like(acc)
    for each in loading:
        each.wait()
    naming.wait()

    def away(w):
        return pltpu.make_async_copy(gone.at[w], answer.at[w], goes.at[w])

    def send(w, carry):
        for j in range(ROOM):
            name = names[w, j]
            asked = jnp.maximum(name, 0)
            b = lax.div(asked, patches)
            gone[w, j * columns : (j + 1) * columns, :] = held[asked]
            chosen = jnp.where(name >= 0, b, n_narrow)
            k = count[chosen]
            count[chosen] = k + 1
            lists[chosen, k] = (w << 16) | (j << 12) | (j << 8) | (asked - b * patches)
        away(w).start()
        return carry

    lax.fori_loop(0, n_wide, send, 0)
    fullest = names[0, ROOM]
    for w in range(1, n_wide):
        fullest = jnp.maximum(fullest, names[w, ROOM])
    mark = jnp.where(fullest > ROOM, MARK, 0.0)
    for b in range(n_narrow):
        lists[b, count[b]] = (META - 1) << 8
    for each in coming:
        each.wait()

    def leave(b):
        return pltpu.make_async_copy(acc.at[b % 4], total.at[pl.ds(b * patches, patches)], outs.at[b % 4])

    for b in range(n_narrow):
        at = b % 4
        if b >= 4:
            leave(b - 4).wait()
            acc[at] = jnp.zeros(acc.shape[1:], jnp.float32)

        def add(k, carry):
            terms = []
            for i in range(2):
                entry = lists[b, 2 * k + i]
                patch = entry & 255
                row = (entry >> 8) & 15
                place = (entry >> 12) & 15
                w = entry >> 16
                value = came[w, pl.ds(pl.multiple_of(place * columns, 16), columns), :].astype(jnp.int32).astype(jnp.float32)
                terms.append((patch, value * scale[w, pl.ds(row, 1), :]))
            for patch, term in terms:
                acc[at, patch] += term
            return carry

        lax.fori_loop(0, lax.div(count[b] + 1, 2), add, 0)
        acc[at, 0, 0:8, 0:128] += jnp.full((8, 128), mark, jnp.float32)
        leave(b).start()
    for w in range(n_wide):
        away(w).wait()
    for b in range(n_narrow - 4, n_narrow):
        leave(b).wait()


def face_kernel(fpatch, slot, arrived, tiles, face, buf, moved, acc, sems, moves, side):
    columns = face.shape[1]
    groups = tiles.shape[0] // GROUP

    def fetch(g):
        for i in range(GROUP):
            spot = slot[g * GROUP + i]
            place = spot & ((1 << SHIFT) - 1)
            pltpu.make_async_copy(
                arrived.at[spot >> SHIFT, pl.ds(pl.multiple_of(place * columns, 16), columns)],
                moved.at[g * GROUP + i],
                moves.at[g],
            ).start()
        tile_copy(tiles, buf, sems, g).start()

    for g in range(AHEAD):
        fetch(g)
    acc[...] = jnp.zeros_like(acc)

    def step(g, carry):
        held = moved.at[pl.ds(g * GROUP, GROUP)]
        pltpu.make_async_copy(held, held, moves.at[g]).wait()
        tile_copy(tiles, buf, sems, g).wait()

        @pl.when(g + AHEAD < groups)
        def _():
            fetch(g + AHEAD)

        for i in range(GROUP):
            p = g * GROUP + i
            acc[fpatch[p]] += lax.dot_general(
                moved[p], buf[p], (((1,), (1,)), ((), ())), preferred_element_type=jnp.float32
            )
        return carry

    lax.fori_loop(0, groups, step, 0)
    out = pltpu.make_async_copy(acc, face, side)
    out.start()
    out.wait()


def shards(disp, loads, tiles, pair_fpatch, pair_sdev, pair_spatch):
    n_wide = lax.axis_size("wide")
    n_narrow = lax.axis_size("narrow")
    pairs, faces, nodes = tiles.shape
    patches, columns, _ = disp.shape
    rows = ROOM * columns + META
    sdev = pair_sdev[:, 0]
    vmem = pl.BlockSpec(memory_space=pltpu.VMEM)
    smem = pl.BlockSpec(memory_space=pltpu.SMEM)
    hbm = pl.BlockSpec(memory_space=pltpu.HBM)
    tile_buf = pltpu.VMEM(tiles.shape, tiles.dtype)
    groups = pairs // GROUP
    part_buf = pltpu.VMEM((2, GROUP, columns, nodes), jnp.float32)
    dma = pltpu.SemaphoreType.DMA
    flops = 2 * pairs * columns * faces * nodes
    table = lax.all_gather(disp, "narrow", axis=0, tiled=True)
    out, slot = pl.pallas_call(
        functools.partial(send_kernel, n_narrow, patches),
        out_shape=(
            jax.ShapeDtypeStruct((n_wide, rows, nodes), jnp.int16),
            jax.ShapeDtypeStruct((pairs,), jnp.int32),
        ),
        in_specs=[smem, smem, smem, vmem, hbm],
        out_specs=(hbm, smem),
        scratch_shapes=[
            tile_buf,
            part_buf,
            pltpu.VMEM((2, GROUP, nodes), jnp.float32),
            pltpu.VMEM((GROUP, nodes), jnp.int32),
            pltpu.VMEM((pairs, columns, nodes), jnp.int16),
            pltpu.VMEM((n_wide, META, nodes), jnp.int32),
            pltpu.VMEM((n_wide, META, nodes), jnp.int16),
            pltpu.SMEM((n_wide,), jnp.int32),
            dma((groups,)),
            dma,
            dma,
        ],
        compiler_params=pltpu.CompilerParams(vmem_limit_bytes=LIMIT),
        cost_estimate=pl.CostEstimate(flops=flops, bytes_accessed=2 * tiles.size, transcendentals=0),
        name="send",
    )(pair_fpatch, sdev, pair_spatch, loads, tiles)
    arrived = lax.all_to_all(out, "wide", split_axis=0, concat_axis=0, tiled=True)
    total, answer = pl.pallas_call(
        functools.partial(turn_kernel, n_narrow),
        out_shape=(
            jax.ShapeDtypeStruct((n_narrow * patches, columns, nodes), jnp.float32),
            jax.ShapeDtypeStruct((n_wide, ROOM * columns, nodes), disp.dtype),
        ),
        in_specs=[hbm, hbm],
        out_specs=(hbm, hbm),
        scratch_shapes=[
            pltpu.VMEM((n_narrow * patches, columns, nodes), disp.dtype),
            pltpu.VMEM((n_wide, ROOM * columns, nodes), disp.dtype),
            pltpu.VMEM((n_wide, rows, nodes), jnp.int16),
            pltpu.VMEM((4, patches, columns, nodes), jnp.float32),
            pltpu.VMEM((n_wide, META, nodes), jnp.float32),
            pltpu.VMEM((n_wide, META, nodes), jnp.int16),
            pltpu.VMEM((n_wide, 128), jnp.int32),
            pltpu.SMEM((n_wide, 128), jnp.int32),
            pltpu.SMEM((n_narrow + 1, n_wide * ROOM + 1), jnp.int32),
            pltpu.SMEM((n_narrow + 1,), jnp.int32),
            dma((n_narrow,)),
            dma((4,)),
            dma((n_wide,)),
            dma((4,)),
            dma,
        ],
        compiler_params=pltpu.CompilerParams(vmem_limit_bytes=LIMIT),
        cost_estimate=pl.CostEstimate(flops=10**7, bytes_accessed=29 * 10**6, transcendentals=0),
        name="turn",
    )(arrived, table)
    back = lax.all_to_all(answer, "wide", split_axis=0, concat_axis=0, tiled=True)
    struct_loads = lax.psum_scatter(total, "narrow", scatter_dimension=0, tiled=True)
    face_disp = pl.pallas_call(
        face_kernel,
        out_shape=jax.ShapeDtypeStruct((loads.shape[0], columns, faces), jnp.float32),
        in_specs=[smem, smem, hbm, hbm],
        out_specs=hbm,
        scratch_shapes=[
            tile_buf,
            pltpu.VMEM((pairs, columns, nodes), disp.dtype),
            pltpu.VMEM((loads.shape[0], columns, faces), jnp.float32),
            dma((groups,)),
            dma((groups,)),
            dma,
        ],
        compiler_params=pltpu.CompilerParams(vmem_limit_bytes=LIMIT),
        cost_estimate=pl.CostEstimate(flops=flops, bytes_accessed=2 * tiles.size, transcendentals=0),
        name="face",
    )(pair_fpatch, slot, back, tiles)
    return lax.cond(
        struct_loads[0, 0, 0] > 1e-7 * MARK,
        lambda f, s: long_way(disp, loads, tiles, pair_fpatch, sdev, pair_spatch),
        lambda f, s: (f, s),
        face_disp,
        struct_loads,
    )


def solution(mesh):
    placed = (
        P(("wide", "narrow"), None, None),
        P(("wide", "narrow"), None, None),
        P(("wide", "narrow"), None, None),
        P(("wide", "narrow")),
        P(("wide", "narrow"), None),
        P(("wide", "narrow")),
    )
    return jax.shard_map(
        shards,
        mesh=mesh,
        in_specs=placed,
        out_specs=(P(("wide", "narrow"), None, None), P(("wide", "narrow"), None, None)),
        check_vma=False,
    )
```

```python
import functools

import jax
import jax.numpy as jnp
from jax import lax
from jax.experimental import pallas as pl
from jax.experimental.pallas import tpu as pltpu
from jax.sharding import PartitionSpec as P

ROOM = 12
FIRM = 8
META = 16
SHIFT = 4
GROUP = 16
AHEAD = 4
STEPS = 128.0
TOP = 32760.0
MARK = 1e37
LIMIT = 63 << 20


def long_way(disp, loads, tiles, pair_fpatch, pair_sdev, pair_spatch):
    n_wide = lax.axis_size("wide")
    n_narrow = lax.axis_size("narrow")
    n_dev = n_wide * n_narrow
    pair_count = tiles.shape[0]
    capacity = max(2, 2 * pair_count // n_dev)
    slot_count = n_dev * capacity
    columns = disp.shape[1]
    node_count = disp.shape[2]
    face_count = loads.shape[2]
    target = pair_sdev
    same_target = target[:, None] == target[None, :]
    earlier = lax.broadcasted_iota(jnp.int32, (pair_count, pair_count), 0) > lax.broadcasted_iota(
        jnp.int32, (pair_count, pair_count), 1
    )
    place = jnp.sum((same_target & earlier).astype(jnp.int32), axis=1)
    slot_of_pair = target * capacity + place
    hits = slot_of_pair[None, :] == jnp.arange(slot_count, dtype=jnp.int32)[:, None]
    filled = jnp.any(hits, axis=1)
    pair_of_slot = jnp.sum(
        jnp.where(hits, jnp.arange(pair_count, dtype=jnp.int32)[None, :], 0), axis=1
    )
    request = jnp.where(filled, pair_spatch[pair_of_slot], -1).reshape(n_dev, capacity)
    asked = lax.all_to_all(request, ("wide", "narrow"), split_axis=0, concat_axis=0, tiled=True)
    wanted = asked >= 0
    picked = disp[jnp.maximum(asked, 0)]
    answer = jnp.where(wanted[:, :, None, None], picked, jnp.zeros_like(picked))
    arrived = lax.all_to_all(answer, ("wide", "narrow"), split_axis=0, concat_axis=0, tiled=True)
    arrived = arrived.reshape(slot_count, columns, node_count)
    moved = arrived[slot_of_pair]
    face_part = jnp.einsum("pcn,pfn->pcf", moved, tiles, preferred_element_type=jnp.float32)
    fluid_onehot = (
        pair_fpatch[None, :] == jnp.arange(loads.shape[0], dtype=jnp.int32)[:, None]
    ).astype(jnp.float32)
    face_disp = jnp.dot(
        fluid_onehot,
        face_part.reshape(pair_count, -1),
        precision=lax.Precision.HIGHEST,
        preferred_element_type=jnp.float32,
    ).reshape(loads.shape[0], columns, face_count)
    pulled = loads[pair_fpatch]
    load_part = jnp.einsum("pcf,pfn->pcn", pulled, tiles, preferred_element_type=jnp.float32)
    outgoing = jnp.where(filled[:, None, None], load_part[pair_of_slot], 0.0).reshape(
        n_dev, capacity, columns, node_count
    )
    returned = lax.all_to_all(outgoing, ("wide", "narrow"), split_axis=0, concat_axis=0, tiled=True)
    returned = returned.reshape(slot_count, columns * node_count)
    struct_onehot = (
        asked.reshape(-1)[None, :] == jnp.arange(disp.shape[0], dtype=jnp.int32)[:, None]
    ).astype(jnp.float32)
    struct_loads = jnp.dot(
        struct_onehot, returned, precision=lax.Precision.HIGHEST, preferred_element_type=jnp.float32
    ).reshape(disp.shape[0], columns, node_count)
    return (face_disp, struct_loads)


def tile_copy(tiles, buf, sems, g):
    part = pl.ds(g * GROUP, GROUP)
    return pltpu.make_async_copy(tiles.at[part], buf.at[part], sems.at[g])


def send_kernel(
    n_narrow, fpatch, sdev, spatch, loads, tiles, disp, out, slot, passed,
    own, buf, parts, most, power, whole, meta, ends, count, sems, side, leaving, keep,
):
    n_wide, patches, columns = out.shape[0], disp.shape[0], whole.shape[1]
    groups = tiles.shape[0] // GROUP
    groups = tiles.shape[0] // GROUP

    for g in range(groups):
        tile_copy(tiles, buf, sems, g).start()
    bring = pltpu.make_async_copy(disp, own, keep.at[0])
    bring.start()
    meta[...] = jnp.zeros_like(meta)
    for w in range(n_wide):
        count[w] = 0
        meta[w, ROOM : ROOM + 1, :] = jnp.full((1, meta.shape[2]), -1, jnp.int32)
    lane = lax.broadcasted_iota(jnp.int32, (1, meta.shape[2]), 1)

    def first(g):
        at = lax.rem(g, 2)
        for i in range(GROUP):
            p = g * GROUP + i
            part = jnp.dot(loads[fpatch[p]], buf[p], preferred_element_type=jnp.float32)
            parts[at, i] = part
            most[at, i : i + 1, :] = jnp.max(jnp.abs(part), axis=0, keepdims=True)

    def second(g):
        at = lax.rem(g, 2)
        steps = jnp.ceil(jnp.log2(jnp.maximum(most[at], 1e-33)) * STEPS)
        unit = TOP * jnp.exp2(steps * (-1.0 / STEPS))
        power[...] = steps.astype(jnp.int32)
        for i in range(GROUP):
            p = g * GROUP + i
            target = sdev[p]
            w = lax.div(target, n_narrow)
            asked = lax.rem(target, n_narrow) * patches + spatch[p]
            seen = count[w]
            count[w] = seen + 1
            place = jnp.minimum(seen, ROOM - 1)
            slot[p] = (w << SHIFT) | place
            rounded = jnp.round(parts[at, i] * unit[i : i + 1, :]).astype(jnp.int32)
            whole[p] = rounded.astype(jnp.int16)
            pltpu.make_async_copy(
                whole.at[p], out.at[w, pl.ds(pl.multiple_of(place * columns, 16), columns)], leaving
            ).start()
            meta[w, pl.ds(place, 1), :] = power[i : i + 1, :]
            names = meta[w, ROOM : ROOM + 1, :]
            meta[w, ROOM : ROOM + 1, :] = jnp.where(lane == place, asked, names)


    tile_copy(tiles, buf, sems, 0).wait()
    first(0)

    def step(g, carry):
        tile_copy(tiles, buf, sems, g).wait()
        first(g)
        second(g - 1)
        return carry

    lax.fori_loop(1, groups, step, 0)
    second(groups - 1)
    bring.wait()
    give = pltpu.make_async_copy(own, passed, keep.at[1])
    give.start()
    fullest = count[0]
    for w in range(1, n_wide):
        fullest = jnp.maximum(fullest, count[w])
    for w in range(n_wide):
        names = meta[w, ROOM : ROOM + 1, :]
        meta[w, ROOM : ROOM + 1, :] = jnp.where(lane == ROOM, fullest, names)
    ends[...] = meta[...].astype(jnp.int16)
    tail = pltpu.make_async_copy(ends, out.at[:, pl.ds(ROOM * columns, META)], side)
    tail.start()
    pltpu.make_async_copy(whole, whole, leaving).wait()
    tail.wait()
    give.wait()


def turn_kernel(
    n_narrow, arrived, table, total, answer,
    held, gone, came, acc, scale, meta, wide_names, names, lists, count, tables, comes, later, goes, rest, outs, side,
):
    n_wide, columns = arrived.shape[0], table.shape[1]
    patches = table.shape[0] // n_narrow
    quarter = n_wide // 4
    ends = pltpu.make_async_copy(arrived.at[:, pl.ds(ROOM * columns, META)], meta, side)
    ends.start()
    loading = [
        pltpu.make_async_copy(
            table.at[pl.ds(b * patches, patches)], held.at[pl.ds(b * patches, patches)], tables.at[b]
        )
        for b in range(n_narrow)
    ]
    coming = [
        pltpu.make_async_copy(
            arrived.at[pl.ds(i * quarter, quarter), pl.ds(0, FIRM * columns)],
            came.at[pl.ds(i * quarter, quarter), pl.ds(0, FIRM * columns)],
            comes.at[i],
        )
        for i in range(4)
    ]
    for each in loading + coming:
        each.start()
    for b in range(n_narrow + 1):
        count[b] = 0
    ends.wait()
    wide_names[...] = meta[...].astype(jnp.int32)[:, ROOM, : wide_names.shape[1]]
    naming = pltpu.make_async_copy(wide_names, names, side)
    naming.start()
    scale[...] = jnp.exp2(meta[...].astype(jnp.int32).astype(jnp.float32) * (1.0 / STEPS)) * (1.0 / TOP)
    scale[0, META - 1 : META, :] = jnp.zeros((1, scale.shape[2]), jnp.float32)
    acc[...] = jnp.zeros_like(acc)
    for each in loading:
        each.wait()
    naming.wait()

    firm, loose = pl.ds(0, FIRM * columns), pl.ds(FIRM * columns, (ROOM - FIRM) * columns)

    def more_come(w):
        return pltpu.make_async_copy(arrived.at[w, loose], came.at[w, loose], later.at[w])

    def away(w):
        return pltpu.make_async_copy(gone.at[w, firm], answer.at[w, firm], goes.at[w])

    def more_away(w):
        return pltpu.make_async_copy(gone.at[w, loose], answer.at[w, loose], rest.at[w])

    def for_full(act):
        def each(w, carry):
            @pl.when(names[w, FIRM] >= 0)
            def _():
                act(w)

            return carry

        lax.fori_loop(0, n_wide, each, 0)

    def serve(w, j):
        name = names[w, j]
        asked = jnp.maximum(name, 0)
        b = lax.div(asked, patches)
        gone[w, j * columns : (j + 1) * columns, :] = held[asked]
        chosen = jnp.where(name >= 0, b, n_narrow)
        k = count[chosen]
        count[chosen] = k + 1
        lists[chosen, k] = (w << 16) | (j << 12) | (j << 8) | (asked - b * patches)

    def send(w, carry):
        for j in range(FIRM):
            serve(w, j)
        away(w).start()

        @pl.when(names[w, FIRM] >= 0)
        def _():
            more_come(w).start()
            for j in range(FIRM, ROOM):
                serve(w, j)
            more_away(w).start()

        return carry

    lax.fori_loop(0, n_wide, send, 0)
    fullest = names[0, ROOM]
    for w in range(1, n_wide):
        fullest = jnp.maximum(fullest, names[w, ROOM])
    mark = jnp.where(fullest > ROOM, MARK, 0.0)
    for b in range(n_narrow):
        lists[b, count[b]] = (META - 1) << 8
    for each in coming:
        each.wait()
    for_full(lambda w: more_come(w).wait())

    def leave(b):
        return pltpu.make_async_copy(acc.at[b % 4], total.at[pl.ds(b * patches, patches)], outs.at[b % 4])

    for b in range(n_narrow):
        at = b % 4
        if b >= 4:
            leave(b - 4).wait()
            acc[at] = jnp.zeros(acc.shape[1:], jnp.float32)

        def add(k, carry):
            terms = []
            for i in range(2):
                entry = lists[b, 2 * k + i]
                patch = entry & 255
                row = (entry >> 8) & 15
                place = (entry >> 12) & 15
                w = entry >> 16
                value = came[w, pl.ds(pl.multiple_of(place * columns, 16), columns), :].astype(jnp.int32).astype(jnp.float32)
                terms.append((patch, value * scale[w, pl.ds(row, 1), :]))
            for patch, term in terms:
                acc[at, patch] += term
            return carry

        lax.fori_loop(0, lax.div(count[b] + 1, 2), add, 0)
        acc[at, 0, 0:8, 0:128] += jnp.full((8, 128), mark, jnp.float32)
        leave(b).start()
    for w in range(n_wide):
        away(w).wait()
    for_full(lambda w: more_away(w).wait())
    for b in range(n_narrow - 4, n_narrow):
        leave(b).wait()


def face_kernel(fpatch, slot, arrived, tiles, face, buf, moved, acc, sems, moves, side):
    columns = face.shape[1]
    groups = tiles.shape[0] // GROUP

    def fetch(g):
        tile_copy(tiles, buf, sems, g).start()
        for i in range(GROUP):
            spot = slot[g * GROUP + i]
            place = spot & ((1 << SHIFT) - 1)
            pltpu.make_async_copy(
                arrived.at[spot >> SHIFT, pl.ds(pl.multiple_of(place * columns, 16), columns)],
                moved.at[g * GROUP + i],
                moves.at[g],
            ).start()

    for g in range(AHEAD):
        fetch(g)
    acc[...] = jnp.zeros_like(acc)

    def step(g, carry):
        held = moved.at[pl.ds(g * GROUP, GROUP)]
        pltpu.make_async_copy(held, held, moves.at[g]).wait()
        tile_copy(tiles, buf, sems, g).wait()

        @pl.when(g + AHEAD < groups)
        def _():
            fetch(g + AHEAD)

        for i in range(GROUP):
            p = g * GROUP + i
            acc[fpatch[p]] += lax.dot_general(
                moved[p], buf[p], (((1,), (1,)), ((), ())), preferred_element_type=jnp.float32
            )
        return carry

    lax.fori_loop(0, groups, step, 0)
    out = pltpu.make_async_copy(acc, face, side)
    out.start()
    out.wait()


def shards(disp, loads, tiles, pair_fpatch, pair_sdev, pair_spatch):
    n_wide = lax.axis_size("wide")
    n_narrow = lax.axis_size("narrow")
    pairs, faces, nodes = tiles.shape
    patches, columns, _ = disp.shape
    rows = ROOM * columns + META
    sdev = pair_sdev[:, 0]
    vmem = pl.BlockSpec(memory_space=pltpu.VMEM)
    smem = pl.BlockSpec(memory_space=pltpu.SMEM)
    hbm = pl.BlockSpec(memory_space=pltpu.HBM)
    tile_buf = pltpu.VMEM(tiles.shape, tiles.dtype)
    groups = pairs // GROUP
    part_buf = pltpu.VMEM((2, GROUP, columns, nodes), jnp.float32)
    dma = pltpu.SemaphoreType.DMA
    flops = 2 * pairs * columns * faces * nodes
    out, slot, passed = pl.pallas_call(
        functools.partial(send_kernel, n_narrow),
        out_shape=(
            jax.ShapeDtypeStruct((n_wide, rows, nodes), jnp.int16),
            jax.ShapeDtypeStruct((pairs,), jnp.int32),
            jax.ShapeDtypeStruct(disp.shape, disp.dtype),
        ),
        in_specs=[smem, smem, smem, vmem, hbm, hbm],
        out_specs=(hbm, smem, hbm),
        scratch_shapes=[
            pltpu.VMEM(disp.shape, disp.dtype),
            tile_buf,
            part_buf,
            pltpu.VMEM((2, GROUP, nodes), jnp.float32),
            pltpu.VMEM((GROUP, nodes), jnp.int32),
            pltpu.VMEM((pairs, columns, nodes), jnp.int16),
            pltpu.VMEM((n_wide, META, nodes), jnp.int32),
            pltpu.VMEM((n_wide, META, nodes), jnp.int16),
            pltpu.SMEM((n_wide,), jnp.int32),
            dma((groups,)),
            dma,
            dma,
            dma((2,)),
        ],
        compiler_params=pltpu.CompilerParams(vmem_limit_bytes=LIMIT),
        cost_estimate=pl.CostEstimate(flops=flops, bytes_accessed=2 * tiles.size, transcendentals=0),
        name="send",
    )(pair_fpatch, sdev, pair_spatch, loads, tiles, disp)
    table = lax.all_gather(passed, "narrow", axis=0, tiled=True)
    arrived = lax.all_to_all(out, "wide", split_axis=0, concat_axis=0, tiled=True)
    total, answer = pl.pallas_call(
        functools.partial(turn_kernel, n_narrow),
        out_shape=(
            jax.ShapeDtypeStruct((n_narrow * patches, columns, nodes), jnp.float32),
            jax.ShapeDtypeStruct((n_wide, ROOM * columns, nodes), disp.dtype),
        ),
        in_specs=[hbm, hbm],
        out_specs=(hbm, hbm),
        scratch_shapes=[
            pltpu.VMEM((n_narrow * patches, columns, nodes), disp.dtype),
            pltpu.VMEM((n_wide, ROOM * columns, nodes), disp.dtype),
            pltpu.VMEM((n_wide, ROOM * columns, nodes), jnp.int16),
            pltpu.VMEM((4, patches, columns, nodes), jnp.float32),
            pltpu.VMEM((n_wide, META, nodes), jnp.float32),
            pltpu.VMEM((n_wide, META, nodes), jnp.int16),
            pltpu.VMEM((n_wide, 128), jnp.int32),
            pltpu.SMEM((n_wide, 128), jnp.int32),
            pltpu.SMEM((n_narrow + 1, n_wide * ROOM + 1), jnp.int32),
            pltpu.SMEM((n_narrow + 1,), jnp.int32),
            dma((n_narrow,)),
            dma((4,)),
            dma((n_wide,)),
            dma((n_wide,)),
            dma((n_wide,)),
            dma((4,)),
            dma,
        ],
        compiler_params=pltpu.CompilerParams(vmem_limit_bytes=LIMIT),
        cost_estimate=pl.CostEstimate(flops=10**7, bytes_accessed=29 * 10**6, transcendentals=0),
        name="turn",
    )(arrived, table)
    back = lax.all_to_all(answer, "wide", split_axis=0, concat_axis=0, tiled=True)
    struct_loads = lax.psum_scatter(total, "narrow", scatter_dimension=0, tiled=True)
    face_disp = pl.pallas_call(
        face_kernel,
        out_shape=jax.ShapeDtypeStruct((loads.shape[0], columns, faces), jnp.float32),
        in_specs=[smem, smem, hbm, hbm],
        out_specs=hbm,
        scratch_shapes=[
            tile_buf,
            pltpu.VMEM((pairs, columns, nodes), disp.dtype),
            pltpu.VMEM((loads.shape[0], columns, faces), jnp.float32),
            dma((groups,)),
            dma((groups,)),
            dma,
        ],
        compiler_params=pltpu.CompilerParams(vmem_limit_bytes=LIMIT),
        cost_estimate=pl.CostEstimate(flops=flops, bytes_accessed=2 * tiles.size, transcendentals=0),
        name="face",
    )(pair_fpatch, slot, back, tiles)
    return lax.cond(
        struct_loads[0, 0, 0] > 1e-7 * MARK,
        lambda f, s: long_way(disp, loads, tiles, pair_fpatch, sdev, pair_spatch),
        lambda f, s: (f, s),
        face_disp,
        struct_loads,
    )


def solution(mesh):
    placed = (
        P(("wide", "narrow"), None, None),
        P(("wide", "narrow"), None, None),
        P(("wide", "narrow"), None, None),
        P(("wide", "narrow")),
        P(("wide", "narrow"), None),
        P(("wide", "narrow")),
    )
    return jax.shard_map(
        shards,
        mesh=mesh,
        in_specs=placed,
        out_specs=(P(("wide", "narrow"), None, None), P(("wide", "narrow"), None, None)),
        check_vma=False,
    )
```

```python
import functools

import jax
import jax.numpy as jnp
from jax import lax
from jax.experimental import pallas as pl
from jax.experimental.pallas import tpu as pltpu
from jax.sharding import PartitionSpec as P

ROOM = 12
FIRM = 8
META = 16
SHIFT = 4
GROUP = 16
AHEAD = 4
STEPS = 128.0
TOP = 32760.0
MARK = 1e37
LIMIT = 255 << 18


def long_way(disp, loads, tiles, pair_fpatch, pair_sdev, pair_spatch):
    n_wide = lax.axis_size("wide")
    n_narrow = lax.axis_size("narrow")
    n_dev = n_wide * n_narrow
    pair_count = tiles.shape[0]
    capacity = max(2, 2 * pair_count // n_dev)
    slot_count = n_dev * capacity
    columns = disp.shape[1]
    node_count = disp.shape[2]
    face_count = loads.shape[2]
    target = pair_sdev
    same_target = target[:, None] == target[None, :]
    earlier = lax.broadcasted_iota(jnp.int32, (pair_count, pair_count), 0) > lax.broadcasted_iota(
        jnp.int32, (pair_count, pair_count), 1
    )
    place = jnp.sum((same_target & earlier).astype(jnp.int32), axis=1)
    slot_of_pair = target * capacity + place
    hits = slot_of_pair[None, :] == jnp.arange(slot_count, dtype=jnp.int32)[:, None]
    filled = jnp.any(hits, axis=1)
    pair_of_slot = jnp.sum(
        jnp.where(hits, jnp.arange(pair_count, dtype=jnp.int32)[None, :], 0), axis=1
    )
    request = jnp.where(filled, pair_spatch[pair_of_slot], -1).reshape(n_dev, capacity)
    asked = lax.all_to_all(request, ("wide", "narrow"), split_axis=0, concat_axis=0, tiled=True)
    wanted = asked >= 0
    picked = disp[jnp.maximum(asked, 0)]
    answer = jnp.where(wanted[:, :, None, None], picked, jnp.zeros_like(picked))
    arrived = lax.all_to_all(answer, ("wide", "narrow"), split_axis=0, concat_axis=0, tiled=True)
    arrived = arrived.reshape(slot_count, columns, node_count)
    moved = arrived[slot_of_pair]
    face_part = jnp.einsum("pcn,pfn->pcf", moved, tiles, preferred_element_type=jnp.float32)
    fluid_onehot = (
        pair_fpatch[None, :] == jnp.arange(loads.shape[0], dtype=jnp.int32)[:, None]
    ).astype(jnp.float32)
    face_disp = jnp.dot(
        fluid_onehot,
        face_part.reshape(pair_count, -1),
        precision=lax.Precision.HIGHEST,
        preferred_element_type=jnp.float32,
    ).reshape(loads.shape[0], columns, face_count)
    pulled = loads[pair_fpatch]
    load_part = jnp.einsum("pcf,pfn->pcn", pulled, tiles, preferred_element_type=jnp.float32)
    outgoing = jnp.where(filled[:, None, None], load_part[pair_of_slot], 0.0).reshape(
        n_dev, capacity, columns, node_count
    )
    returned = lax.all_to_all(outgoing, ("wide", "narrow"), split_axis=0, concat_axis=0, tiled=True)
    returned = returned.reshape(slot_count, columns * node_count)
    struct_onehot = (
        asked.reshape(-1)[None, :] == jnp.arange(disp.shape[0], dtype=jnp.int32)[:, None]
    ).astype(jnp.float32)
    struct_loads = jnp.dot(
        struct_onehot, returned, precision=lax.Precision.HIGHEST, preferred_element_type=jnp.float32
    ).reshape(disp.shape[0], columns, node_count)
    return (face_disp, struct_loads)


def tile_copy(tiles, buf, sems, g):
    part = pl.ds(g * GROUP, GROUP)
    return pltpu.make_async_copy(tiles.at[part], buf.at[part], sems.at[g])


def send_kernel(
    n_narrow, fpatch, sdev, spatch, loads, tiles, disp, out, slot, passed,
    own, buf, power, whole, meta, ends, count, sems, side, leaving, keep,
):
    n_wide, patches, columns = out.shape[0], disp.shape[0], whole.shape[1]
    groups = tiles.shape[0] // GROUP
    groups = tiles.shape[0] // GROUP

    for g in range(groups):
        tile_copy(tiles, buf, sems, g).start()
    bring = pltpu.make_async_copy(disp, own, keep.at[0])
    bring.start()
    meta[...] = jnp.zeros_like(meta)
    for w in range(n_wide):
        count[w] = 0
        meta[w, ROOM : ROOM + 1, :] = jnp.full((1, meta.shape[2]), -1, jnp.int32)
    lane = lax.broadcasted_iota(jnp.int32, (1, meta.shape[2]), 1)

    def first(g):
        at = lax.rem(g, 2)
        for i in range(GROUP):
            p = g * GROUP + i
            part = jnp.dot(loads[fpatch[p]], buf[p], preferred_element_type=jnp.float32)
            most = jnp.max(jnp.abs(part), axis=0, keepdims=True)
            steps = jnp.ceil(jnp.log2(jnp.maximum(most, 1e-33)) * STEPS)
            unit = TOP * jnp.exp2(steps * (-1.0 / STEPS))
            whole[p] = jnp.round(part * unit).astype(jnp.int32).astype(jnp.int16)
            power[at, i : i + 1, :] = steps.astype(jnp.int32)

    def second(g):
        at = lax.rem(g, 2)
        for i in range(GROUP):
            p = g * GROUP + i
            target = sdev[p]
            w = lax.div(target, n_narrow)
            asked = lax.rem(target, n_narrow) * patches + spatch[p]
            seen = count[w]
            count[w] = seen + 1
            place = jnp.minimum(seen, ROOM - 1)
            slot[p] = (w << SHIFT) | place
            pltpu.make_async_copy(
                whole.at[p], out.at[w, pl.ds(pl.multiple_of(place * columns, 16), columns)], leaving
            ).start()
            meta[w, pl.ds(place, 1), :] = power[at, i : i + 1, :]
            names = meta[w, ROOM : ROOM + 1, :]
            meta[w, ROOM : ROOM + 1, :] = jnp.where(lane == place, asked, names)


    tile_copy(tiles, buf, sems, 0).wait()
    first(0)

    def step(g, carry):
        tile_copy(tiles, buf, sems, g).wait()
        first(g)
        second(g - 1)
        return carry

    lax.fori_loop(1, groups, step, 0)
    second(groups - 1)
    bring.wait()
    give = pltpu.make_async_copy(own, passed, keep.at[1])
    give.start()
    fullest = count[0]
    for w in range(1, n_wide):
        fullest = jnp.maximum(fullest, count[w])
    for w in range(n_wide):
        names = meta[w, ROOM : ROOM + 1, :]
        meta[w, ROOM : ROOM + 1, :] = jnp.where(lane == ROOM, fullest, names)
    ends[...] = meta[...].astype(jnp.int16)
    tail = pltpu.make_async_copy(ends, out.at[:, pl.ds(ROOM * columns, META)], side)
    tail.start()
    pltpu.make_async_copy(whole, whole, leaving).wait()
    tail.wait()
    give.wait()


def turn_kernel(
    n_narrow, arrived, table, total, answer,
    held, gone, came, acc, scale, meta, wide_names, names, lists, count, tables, comes, later, goes, rest, outs, side,
):
    n_wide, columns = arrived.shape[0], table.shape[1]
    patches = table.shape[0] // n_narrow
    quarter = n_wide // 4
    ends = pltpu.make_async_copy(arrived.at[:, pl.ds(ROOM * columns, META)], meta, side)
    ends.start()
    loading = [
        pltpu.make_async_copy(
            table.at[pl.ds(b * patches, patches)], held.at[pl.ds(b * patches, patches)], tables.at[b]
        )
        for b in range(n_narrow)
    ]
    coming = [
        pltpu.make_async_copy(
            arrived.at[pl.ds(i * quarter, quarter), pl.ds(0, FIRM * columns)],
            came.at[pl.ds(i * quarter, quarter), pl.ds(0, FIRM * columns)],
            comes.at[i],
        )
        for i in range(4)
    ]
    for each in loading + coming:
        each.start()
    for b in range(n_narrow + 1):
        count[b] = 0
    ends.wait()
    wide_names[...] = meta[...].astype(jnp.int32)[:, ROOM, : wide_names.shape[1]]
    naming = pltpu.make_async_copy(wide_names, names, side)
    naming.start()
    scale[...] = jnp.exp2(meta[...].astype(jnp.int32).astype(jnp.float32) * (1.0 / STEPS)) * (1.0 / TOP)
    scale[0, META - 1 : META, :] = jnp.zeros((1, scale.shape[2]), jnp.float32)
    acc[...] = jnp.zeros_like(acc)
    for each in loading:
        each.wait()
    naming.wait()

    firm, loose = pl.ds(0, FIRM * columns), pl.ds(FIRM * columns, (ROOM - FIRM) * columns)

    def more_come(w):
        return pltpu.make_async_copy(arrived.at[w, loose], came.at[w, loose], later.at[w])

    def away(w):
        return pltpu.make_async_copy(gone.at[w, firm], answer.at[w, firm], goes.at[w])

    def more_away(w):
        return pltpu.make_async_copy(gone.at[w, loose], answer.at[w, loose], rest.at[w])

    def for_full(act):
        def each(w, carry):
            @pl.when(names[w, FIRM] >= 0)
            def _():
                act(w)

            return carry

        lax.fori_loop(0, n_wide, each, 0)

    def serve(w, j):
        name = names[w, j]
        asked = jnp.maximum(name, 0)
        b = lax.div(asked, patches)
        gone[w, j * columns : (j + 1) * columns, :] = held[asked]
        chosen = jnp.where(name >= 0, b, n_narrow)
        k = count[chosen]
        count[chosen] = k + 1
        lists[chosen, k] = (w << 16) | (j << 12) | (j << 8) | (asked - b * patches)

    def send(w, carry):
        for j in range(FIRM):
            serve(w, j)
        away(w).start()

        @pl.when(names[w, FIRM] >= 0)
        def _():
            more_come(w).start()
            for j in range(FIRM, ROOM):
                serve(w, j)
            more_away(w).start()

        return carry

    lax.fori_loop(0, n_wide, send, 0)
    fullest = names[0, ROOM]
    for w in range(1, n_wide):
        fullest = jnp.maximum(fullest, names[w, ROOM])
    mark = jnp.where(fullest > ROOM, MARK, 0.0)
    for b in range(n_narrow):
        lists[b, count[b]] = (META - 1) << 8
    for each in coming:
        each.wait()
    for_full(lambda w: more_come(w).wait())

    def leave(b):
        return pltpu.make_async_copy(acc.at[b % 4], total.at[pl.ds(b * patches, patches)], outs.at[b % 4])

    for b in range(n_narrow):
        at = b % 4
        if b >= 4:
            leave(b - 4).wait()
            acc[at] = jnp.zeros(acc.shape[1:], jnp.float32)

        def add(k, carry):
            terms = []
            for i in range(2):
                entry = lists[b, 2 * k + i]
                patch = entry & 255
                row = (entry >> 8) & 15
                place = (entry >> 12) & 15
                w = entry >> 16
                value = came[w, pl.ds(pl.multiple_of(place * columns, 16), columns), :].astype(jnp.int32).astype(jnp.float32)
                terms.append((patch, value * scale[w, pl.ds(row, 1), :]))
            for patch, term in terms:
                acc[at, patch] += term
            return carry

        lax.fori_loop(0, lax.div(count[b] + 1, 2), add, 0)
        acc[at, 0, 0:8, 0:128] += jnp.full((8, 128), mark, jnp.float32)
        leave(b).start()
    for w in range(n_wide):
        away(w).wait()
    for_full(lambda w: more_away(w).wait())
    for b in range(n_narrow - 4, n_narrow):
        leave(b).wait()


def face_kernel(fpatch, slot, arrived, tiles, face, buf, moved, acc, sems, moves, side):
    columns = face.shape[1]
    groups = tiles.shape[0] // GROUP

    def fetch(g):
        tile_copy(tiles, buf, sems, g).start()
        for i in range(GROUP):
            spot = slot[g * GROUP + i]
            place = spot & ((1 << SHIFT) - 1)
            pltpu.make_async_copy(
                arrived.at[spot >> SHIFT, pl.ds(pl.multiple_of(place * columns, 16), columns)],
                moved.at[g * GROUP + i],
                moves.at[g],
            ).start()

    for g in range(AHEAD):
        fetch(g)
    acc[...] = jnp.zeros_like(acc)

    def step(g, carry):
        held = moved.at[pl.ds(g * GROUP, GROUP)]
        pltpu.make_async_copy(held, held, moves.at[g]).wait()
        tile_copy(tiles, buf, sems, g).wait()

        @pl.when(g + AHEAD < groups)
        def _():
            fetch(g + AHEAD)

        for i in range(GROUP):
            p = g * GROUP + i
            acc[fpatch[p]] += lax.dot_general(
                moved[p], buf[p], (((1,), (1,)), ((), ())), preferred_element_type=jnp.float32
            )
        return carry

    lax.fori_loop(0, groups, step, 0)
    out = pltpu.make_async_copy(acc, face, side)
    out.start()
    out.wait()


def shards(disp, loads, tiles, pair_fpatch, pair_sdev, pair_spatch):
    n_wide = lax.axis_size("wide")
    n_narrow = lax.axis_size("narrow")
    pairs, faces, nodes = tiles.shape
    patches, columns, _ = disp.shape
    rows = ROOM * columns + META
    sdev = pair_sdev[:, 0]
    vmem = pl.BlockSpec(memory_space=pltpu.VMEM)
    smem = pl.BlockSpec(memory_space=pltpu.SMEM)
    hbm = pl.BlockSpec(memory_space=pltpu.HBM)
    tile_buf = pltpu.VMEM(tiles.shape, tiles.dtype)
    groups = pairs // GROUP
    dma = pltpu.SemaphoreType.DMA
    flops = 2 * pairs * columns * faces * nodes
    out, slot, passed = pl.pallas_call(
        functools.partial(send_kernel, n_narrow),
        out_shape=(
            jax.ShapeDtypeStruct((n_wide, rows, nodes), jnp.int16),
            jax.ShapeDtypeStruct((pairs,), jnp.int32),
            jax.ShapeDtypeStruct(disp.shape, disp.dtype),
        ),
        in_specs=[smem, smem, smem, vmem, hbm, hbm],
        out_specs=(hbm, smem, hbm),
        scratch_shapes=[
            pltpu.VMEM(disp.shape, disp.dtype),
            tile_buf,
            pltpu.VMEM((2, GROUP, nodes), jnp.int32),
            pltpu.VMEM((pairs, columns, nodes), jnp.int16),
            pltpu.VMEM((n_wide, META, nodes), jnp.int32),
            pltpu.VMEM((n_wide, META, nodes), jnp.int16),
            pltpu.SMEM((n_wide,), jnp.int32),
            dma((groups,)),
            dma,
            dma,
            dma((2,)),
        ],
        compiler_params=pltpu.CompilerParams(vmem_limit_bytes=LIMIT),
        cost_estimate=pl.CostEstimate(flops=flops, bytes_accessed=2 * tiles.size, transcendentals=0),
        name="send",
    )(pair_fpatch, sdev, pair_spatch, loads, tiles, disp)
    table = lax.all_gather(passed, "narrow", axis=0, tiled=True)
    arrived = lax.all_to_all(out, "wide", split_axis=0, concat_axis=0, tiled=True)
    total, answer = pl.pallas_call(
        functools.partial(turn_kernel, n_narrow),
        out_shape=(
            jax.ShapeDtypeStruct((n_narrow * patches, columns, nodes), jnp.float32),
            jax.ShapeDtypeStruct((n_wide, ROOM * columns, nodes), disp.dtype),
        ),
        in_specs=[hbm, hbm],
        out_specs=(hbm, hbm),
        scratch_shapes=[
            pltpu.VMEM((n_narrow * patches, columns, nodes), disp.dtype),
            pltpu.VMEM((n_wide, ROOM * columns, nodes), disp.dtype),
            pltpu.VMEM((n_wide, ROOM * columns, nodes), jnp.int16),
            pltpu.VMEM((4, patches, columns, nodes), jnp.float32),
            pltpu.VMEM((n_wide, META, nodes), jnp.float32),
            pltpu.VMEM((n_wide, META, nodes), jnp.int16),
            pltpu.VMEM((n_wide, 128), jnp.int32),
            pltpu.SMEM((n_wide, 128), jnp.int32),
            pltpu.SMEM((n_narrow + 1, n_wide * ROOM + 1), jnp.int32),
            pltpu.SMEM((n_narrow + 1,), jnp.int32),
            dma((n_narrow,)),
            dma((4,)),
            dma((n_wide,)),
            dma((n_wide,)),
            dma((n_wide,)),
            dma((4,)),
            dma,
        ],
        compiler_params=pltpu.CompilerParams(vmem_limit_bytes=LIMIT),
        cost_estimate=pl.CostEstimate(flops=10**7, bytes_accessed=29 * 10**6, transcendentals=0),
        name="turn",
    )(arrived, table)
    back = lax.all_to_all(answer, "wide", split_axis=0, concat_axis=0, tiled=True)
    struct_loads = lax.psum_scatter(total, "narrow", scatter_dimension=0, tiled=True)
    face_disp = pl.pallas_call(
        face_kernel,
        out_shape=jax.ShapeDtypeStruct((loads.shape[0], columns, faces), jnp.float32),
        in_specs=[smem, smem, hbm, hbm],
        out_specs=hbm,
        scratch_shapes=[
            tile_buf,
            pltpu.VMEM((pairs, columns, nodes), disp.dtype),
            pltpu.VMEM((loads.shape[0], columns, faces), jnp.float32),
            dma((groups,)),
            dma((groups,)),
            dma,
        ],
        compiler_params=pltpu.CompilerParams(vmem_limit_bytes=LIMIT),
        cost_estimate=pl.CostEstimate(flops=flops, bytes_accessed=2 * tiles.size, transcendentals=0),
        name="face",
    )(pair_fpatch, slot, back, tiles)
    return lax.cond(
        struct_loads[0, 0, 0] > 1e-7 * MARK,
        lambda f, s: long_way(disp, loads, tiles, pair_fpatch, sdev, pair_spatch),
        lambda f, s: (f, s),
        face_disp,
        struct_loads,
    )


def solution(mesh):
    placed = (
        P(("wide", "narrow"), None, None),
        P(("wide", "narrow"), None, None),
        P(("wide", "narrow"), None, None),
        P(("wide", "narrow")),
        P(("wide", "narrow"), None),
        P(("wide", "narrow")),
    )
    return jax.shard_map(
        shards,
        mesh=mesh,
        in_specs=placed,
        out_specs=(P(("wide", "narrow"), None, None), P(("wide", "narrow"), None, None)),
        check_vma=False,
    )
```
